512 devices in a mesh: ctx: 64 (over x, y, core), sess: 8 (over z).
Axes of the slice: x: 4, y: 8, z: 8, core: 2. Of those that a mesh axis runs over, the one named last changes fastest.
Arguments:
- hidden_slab: bfloat16 [8, 4096, 5120], P('sess', 'ctx'), may hold values from -6 to 6
- projection: bfloat16 [5120, 1024], P(('ctx', 'sess')), may hold values from -0.078125 to 0.078125
- adapter_down: bfloat16 [8, 5120, 64], P('sess'), may hold values from -0.078125 to 0.078125
- adapter_up: bfloat16 [8, 2, 32, 512], P('sess'), may hold values from -1 to 1
- key_gain: float32 [128], replicated, may hold values from 0.5 to 2
- cache_keys: bfloat16 [8, 8192, 512], P('sess', 'ctx'), may hold values from -4 to 4
- cache_values: bfloat16 [8, 8192, 512], P('sess', 'ctx'), may hold values from -6 to 6
- fresh_keys: bfloat16 [8, 64, 512], P('sess', 'ctx'), may hold values from -4 to 4
- fresh_values: bfloat16 [8, 64, 512], P('sess', 'ctx'), may hold values from -6 to 6
- queries: bfloat16 [8, 64, 4096], P('sess', 'ctx'), may hold values from -24 to 24
- slab_length: int32 [8], P('sess'), may hold values from 512 to 4096, as said below
- cache_length: int32 [8, 64], P('sess', 'ctx'), may hold values from 1 to 128, as said below
Outputs:
- slab_cache: bfloat16 [8, 4096, 1024], P('sess', 'ctx')
- attended: bfloat16 [8, 64, 4096], P('sess', 'ctx')
The draws below stay inside these ranges and needn't reach their ends.
Inputs may be any that keep to these rules, and one draw needn't show every extreme that they name: `slab_length`: some session has exactly 4096 live prefix rows. `cache_length`: in every session some context shard has all 128 slots filled.
All inputs are finite; a program needn't handle non-finite values.
Results may differ from the reference program's by a relative error of at most 0.012.
Values may be sent and summed in bfloat16 or wider, within the bound.
No kernel may reach another device: no remote copies, remote signals or barrier semaphores. Data moves between devices by JAX's collectives and lax.ppermute only.
A program may use at most 128 MiB of HBM per device.

```python
import math
import jax
import jax.numpy as jnp
from jax import lax

D = 5120
KVH = 4
QH = 32
HD = 128
RANK = 32
SLAB_DEV = 64
CACHE_DEV = 128
NEW_DEV = 1
SESSIONS = 8
SLAB = 4096
CONTEXT = 8192
NEW_TOK = 64
BLOCK = 1
N_CTX = 64


def draw_queries(key, part):
    key = jax.random.fold_in(key, 11)
    shape = (SESSIONS, NEW_TOK, QH * HD)
    values = jnp.clip(3.0 * jax.random.normal(key, shape, jnp.float32), -18.0, 18.0)
    return values.astype(jnp.bfloat16)


def draw_cache_keys(key, part):
    key = jax.random.fold_in(key, 12)
    shape = (SESSIONS, CONTEXT, KVH * HD)
    values = jnp.clip(jax.random.normal(key, shape, jnp.float32), -4.0, 4.0)
    return values.astype(jnp.bfloat16)


def draw_slab_length(key, part):
    key = jax.random.fold_in(key, 14)
    first, second = jax.random.split(key)
    lengths = jax.random.randint(first, (SESSIONS,), SLAB // 8, SLAB + 1)
    fullest = jax.random.randint(second, (), 0, SESSIONS)
    return jnp.where(jnp.arange(SESSIONS) == fullest, SLAB, lengths).astype(jnp.int32)


def draw_cache_length(key, part):
    key = jax.random.fold_in(key, 13)
    first, second = jax.random.split(key)
    lengths = jax.random.randint(first, (SESSIONS, N_CTX), 1, CACHE_DEV + 1)
    fullest = jax.random.randint(second, (SESSIONS,), 0, N_CTX)
    chosen = jnp.arange(N_CTX)[None, :] == fullest[:, None]
    return jnp.where(chosen, CACHE_DEV, lengths).astype(jnp.int32)


def level_of(stream_key, shape, cuts, smallest, top_value):
    factor_of = 1.0
    for axis_at, parts in cuts:
        steps = jax.random.uniform(jax.random.fold_in(jax.random.fold_in(stream_key, 6), axis_at), (parts,), jnp.float32, smallest / len(cuts), top_value / len(cuts))
        factor_of = factor_of * jnp.repeat(jnp.exp(steps), shape[axis_at] // parts).reshape((-1,) + (1,) * (len(shape) - 1 - axis_at))
    return factor_of


def centred(own_key, shape, deviation, reach, pieces=(), kind=jnp.bfloat16):
    values = deviation * jax.random.normal(own_key, shape, jnp.float32)
    if pieces:
        values = values * level_of(own_key, shape, pieces, -0.22, 0.18)
    return jnp.clip(values, -reach, reach).astype(kind)


def setup_inputs(seed: int = 0) -> dict:
    seeds = jax.random.split(jax.random.key(seed), 13)
    return {
        "hidden_slab": centred(seeds[0], (SESSIONS, SLAB, D), 1.0, 6.0, ((0, 8), (1, 64))),
        "projection": centred(seeds[1], (D, 2 * KVH * HD), D ** -0.5, 0.078125, ((0, 512),)),
        "adapter_down": centred(seeds[2], (SESSIONS, D, 2 * RANK), D ** -0.5, 0.078125, ((0, 8),)),
        "adapter_up": centred(seeds[3], (SESSIONS, 2, RANK, KVH * HD), RANK ** -0.5, 1.0, ((0, 8),)),
        "key_gain": jnp.clip(jnp.exp(jax.random.uniform(seeds[4], (HD,), jnp.float32, math.log(0.5), math.log(2.0))), 0.5, 2.0),
        "cache_keys": draw_cache_keys(jax.random.fold_in(seeds[12], 71), 0),
        "cache_values": centred(seeds[6], (SESSIONS, CONTEXT, KVH * HD), 1.0, 6.0, ((0, 8), (1, 64))),
        "fresh_keys": centred(seeds[7], (SESSIONS, NEW_TOK, KVH * HD), 1.0, 4.0, ((0, 8), (1, 64))),
        "fresh_values": centred(seeds[8], (SESSIONS, NEW_TOK, KVH * HD), 1.0, 6.0, ((0, 8), (1, 64))),
        "queries": draw_queries(jax.random.fold_in(seeds[12], 71), 0),
        "slab_length": draw_slab_length(jax.random.fold_in(seeds[12], 71), 0),
        "cache_length": draw_cache_length(jax.random.fold_in(seeds[12], 71), 0),
    }


adapter_scale = 0.5
norm_epsilon = 1e-06

def finish_rows(base_part, slab_rows, down_part, up_part, key_gain):
    row_count = slab_rows.shape[0]
    low_rank = up_part.shape[1]
    half_width = base_part.shape[1] // 2
    head_size = key_gain.shape[0]
    low_part = jnp.dot(slab_rows, down_part, preferred_element_type=jnp.float32).astype(jnp.bfloat16)
    delta_keys = jnp.dot(low_part[:, :low_rank], up_part[0], preferred_element_type=jnp.float32)
    delta_values = jnp.dot(low_part[:, low_rank:], up_part[1], preferred_element_type=jnp.float32)
    projected = base_part + adapter_scale * jnp.concatenate([delta_keys, delta_values], axis=1)
    raw_keys = projected[:, :half_width].reshape(row_count, half_width // head_size, head_size)
    normed = raw_keys * lax.rsqrt(lax.optimization_barrier(jnp.mean(raw_keys * raw_keys, axis=-1, keepdims=True)) + norm_epsilon) * key_gain
    new_keys = normed.reshape(row_count, half_width).astype(jnp.bfloat16)
    new_values = projected[:, half_width:].astype(jnp.bfloat16)
    return jnp.concatenate([new_keys, new_values], axis=1)

def session_attention(query_grid, cache_k, cache_v, slab_k, slab_v, fresh_k, fresh_v, cache_counts, slab_usable):
    scale = 1.0 / math.sqrt(HD)
    query_pos = jnp.arange(NEW_TOK)

    def step(carry, inputs):
        ck, cv, sk, sv, fk, fv, cache_count, slab_ok, shard_index = inputs
        all_keys = jnp.concatenate([ck, sk, fk], axis=0).astype(jnp.float32).reshape(-1, KVH, HD)
        all_values = jnp.concatenate([cv, sv, fv], axis=0).astype(jnp.float32).reshape(-1, KVH, HD)
        scores = jnp.einsum('qkgd,nkd->kgqn', query_grid, all_keys) * scale
        cache_ok = jnp.arange(CACHE_DEV) < cache_count
        fresh_pos = shard_index * NEW_DEV + jnp.arange(NEW_DEV)
        usable = jnp.concatenate([jnp.broadcast_to(cache_ok[None, :], (NEW_TOK, CACHE_DEV)), jnp.broadcast_to(slab_ok[None, :], (NEW_TOK, SLAB_DEV)), fresh_pos[None, :] <= query_pos[:, None]], axis=1)
        masked = jnp.where(usable[None, None], scores, -jnp.inf)
        row_max = lax.optimization_barrier(jnp.max(masked, axis=-1))
        weights = jnp.exp(masked - row_max[..., None]).astype(jnp.bfloat16)
        weights_wide = weights.astype(jnp.float32)
        row_total = lax.optimization_barrier(jnp.sum(weights_wide, axis=-1))
        row_output = jnp.einsum('kgqn,nkd->kgqd', weights_wide, all_values)
        return (carry, (row_max, row_total, row_output))
    inputs = (cache_k, cache_v, slab_k, slab_v, fresh_k, fresh_v, cache_counts, slab_usable, jnp.arange(N_CTX))
    unused, (maxima, totals, outputs) = lax.scan(step, jnp.zeros((), jnp.float32), inputs)
    largest = lax.optimization_barrier(jnp.max(maxima, axis=0))
    factor = jnp.exp(maxima - largest)
    merged_total = lax.optimization_barrier(jnp.sum(factor * totals, axis=0))
    merged_output = lax.optimization_barrier(jnp.sum(factor[..., None] * outputs, axis=0))
    result = merged_output / merged_total[..., None]
    return result.transpose(2, 0, 1, 3).reshape(NEW_TOK, QH * HD).astype(jnp.bfloat16)

def reference(hidden_slab, projection, adapter_down, adapter_up, key_gain, cache_keys, cache_values, fresh_keys, fresh_values, queries, slab_length, cache_length):
    width = KVH * HD
    group_size = QH // KVH
    caches = []
    answers = []
    for session in range(SESSIONS):
        slab_rows = hidden_slab[session]
        base_part = jnp.dot(slab_rows, projection, preferred_element_type=jnp.float32)
        rebuilt = finish_rows(base_part, slab_rows, adapter_down[session], adapter_up[session], key_gain)
        placed = rebuilt.reshape(N_CTX, N_CTX, BLOCK, 2 * width).transpose(1, 0, 2, 3).reshape(SLAB, 2 * width)
        initial = jnp.arange(SLAB).reshape(N_CTX, N_CTX, BLOCK).transpose(1, 0, 2).reshape(SLAB)
        slab_usable = (initial < slab_length[session]).reshape(N_CTX, SLAB_DEV)
        caches.append(placed)
        query_grid = queries[session].astype(jnp.float32).reshape(NEW_TOK, KVH, group_size, HD)
        answers.append(session_attention(query_grid, cache_keys[session].reshape(N_CTX, CACHE_DEV, width), cache_values[session].reshape(N_CTX, CACHE_DEV, width), placed[:, :width].reshape(N_CTX, SLAB_DEV, width), placed[:, width:].reshape(N_CTX, SLAB_DEV, width), fresh_keys[session].reshape(N_CTX, NEW_DEV, width), fresh_values[session].reshape(N_CTX, NEW_DEV, width), cache_length[session], slab_usable))
    return (jnp.stack(caches), jnp.stack(answers))
```

```python
import functools
import math

import jax
import jax.numpy as jnp
from jax import lax
from jax.experimental import pallas as pl
from jax.experimental.pallas import tpu as pltpu
from jax.sharding import Mesh, PartitionSpec as P

adapter_scale = 0.5
norm_epsilon = 1e-06
masked_score = -1e30
HD = 128
NX, NY, NC, NZ = 4, 8, 2, 8
CTX = ("x", "y", "c")
bf16 = jnp.bfloat16
f32 = jnp.float32


def dot_nt(a, b):
    return lax.dot_general(a, b, (((1,), (1,)), ((), ())), preferred_element_type=f32)


def dot_nn(a, b):
    return lax.dot_general(a, b, (((1,), (0,)), ((), ())), preferred_element_type=f32)


def rebuild_attend(
    place, weight, hidden, down, up, gain, context, out, base, low, asked
):
    step = pl.program_id(0)

    @pl.when(step == 0)
    def _():
        base[...] = jnp.zeros_like(base)
        low[...] = jnp.zeros_like(low)

    rows = hidden[...].reshape(NX * 64, 1280)
    key_weight = weight[:, :, 0:80, :].reshape(1280, HD)
    value_weight = weight[:, :, 80:160, :].reshape(1280, HD)
    base[:, 0:HD] += dot_nn(rows, key_weight)
    base[:, HD:] += dot_nn(rows, value_weight)
    low[...] += dot_nt(rows, down[...])
    tail = weight[:, :, 160:176, :].astype(f32)
    asked[step] = tail[:, :, 0:8, :].reshape(NY * NC * 8, HD)

    @pl.when(step == NX - 1)
    def _():
        slab_length = place[0]
        y = place[1]
        c = place[2]
        projected = base[...] + adapter_scale * dot_nn(low[...].astype(bf16), up[...])
        raw_keys = projected[:, 0:HD]
        mean = jnp.mean(raw_keys * raw_keys, axis=-1, keepdims=True)
        new_keys = (raw_keys * lax.rsqrt(mean + norm_epsilon) * gain[...]).astype(bf16)
        new_values = projected[:, HD:].astype(bf16)
        queries = asked[...].reshape(512, HD).astype(bf16)

        column = lax.broadcasted_iota(jnp.int32, (1, 256), 1)
        initial = (column >> 6) * 1024 + (y * 2 + c) * 64 + (column & 63)
        slab_scores = jnp.where(
            initial < slab_length, dot_nt(queries, new_keys), masked_score
        )
        cache_keys = context[:, 0:128, :].reshape(512, HD)
        cache_values = context[:, 128:256, :].reshape(512, HD)
        lane = lax.broadcasted_iota(jnp.int32, (1, HD), 1).astype(f32)
        filled = jnp.concatenate(
            [
                jnp.where(lane < context[i, 256:272, :].astype(f32)[1:2, :], 1.0, 0.0)
                for i in range(NX)
            ],
            axis=1,
        )
        cache_scores = jnp.where(
            filled > 0.5, dot_nt(queries, cache_keys), masked_score
        )
        fresh_keys = context[:, 256:272, :].reshape(64, HD)
        fresh_values = context[:, 272:288, :].reshape(64, HD)
        token = lax.broadcasted_iota(jnp.int32, (512, 64), 0) >> 3
        fresh = lax.broadcasted_iota(jnp.int32, (512, 64), 1)
        fresh_pos = (fresh >> 4) * 16 + y * 2 + c
        fresh_ok = ((fresh & 15) == 0) & (fresh_pos <= token)
        fresh_scores = jnp.where(fresh_ok, dot_nt(queries, fresh_keys), masked_score)

        scale = 1.0 / math.sqrt(HD)
        row_max = jnp.maximum(
            jnp.maximum(
                jnp.max(slab_scores, axis=-1, keepdims=True),
                jnp.max(cache_scores, axis=-1, keepdims=True),
            ),
            jnp.max(fresh_scores, axis=-1, keepdims=True),
        )
        shift = (row_max * scale).astype(bf16).astype(f32)

        def weigh(scores, values):
            weights = jnp.exp(scores * scale - shift).astype(bf16)
            wide = jnp.concatenate([values, jnp.ones_like(values)], axis=1)
            return dot_nn(weights, wide)

        merged = (
            weigh(slab_scores, new_values)
            + weigh(cache_scores, cache_values)
            + weigh(fresh_scores, fresh_values)
        )
        total = merged[:, HD:]
        high = total.astype(bf16).astype(f32)
        lanes = lax.broadcasted_iota(jnp.int32, (512, HD), 1)
        stats = jnp.where(
            lanes == 0, shift, jnp.where(lanes == 1, high, total - high)
        )
        target = lax.broadcasted_iota(jnp.int32, (512, 1), 0)
        origin = (target & 1) * 256 + ((target >> 1) & 3) * 64 + (target >> 3)
        pick = jnp.where(
            lax.broadcasted_iota(jnp.int32, (512, 512), 1) == origin, 1.0, 0.0
        ).astype(bf16)
        spread = dot_nn(pick, jnp.concatenate([new_keys, new_values], axis=0))
        out[:, 0:HD] = merged[:, 0:HD].astype(bf16)
        out[:, HD : 2 * HD] = stats.astype(bf16)
        out[:, 2 * HD :] = spread.astype(bf16)


def merge(parts, slab, attended):
    heads = []
    rebuilt = []
    for h in range(NX):
        block = parts[h * 128 : (h + 1) * 128, :]
        output = block[:, 0:HD].astype(f32).reshape(16, 8, HD)
        stats = block[:, HD : 2 * HD].astype(f32).reshape(16, 8, HD)
        rebuilt.append(block[:, 2 * HD :])
        shift = stats[:, :, 0:1]
        total = stats[:, :, 1:2] + stats[:, :, 2:3]
        largest = jnp.max(shift, axis=0, keepdims=True)
        factor = jnp.exp(shift - largest)
        merged_total = jnp.sum(factor * total, axis=0)
        merged_output = jnp.sum(factor * output, axis=0)
        heads.append(merged_output / merged_total)
    attended[...] = jnp.concatenate(heads, axis=0).astype(bf16)
    target = lax.broadcasted_iota(jnp.int32, (128, 1), 0)
    origin = (target & 15) * 8 + ((target >> 4) & 3) * 2 + (target >> 6)
    pick = jnp.where(
        lax.broadcasted_iota(jnp.int32, (128, 128), 1) == origin, 1.0, 0.0
    ).astype(bf16)
    placed = dot_nn(pick, jnp.concatenate(rebuilt, axis=1)).astype(bf16)
    slab[:, 0:512] = placed[0:64, :]
    slab[:, 512:1024] = placed[64:128, :]


def broadcast_over(value, axis):
    size = lax.axis_size(axis)
    return lax.all_to_all(
        jnp.broadcast_to(value[None], (size,) + value.shape), axis, 0, 0, tiled=True
    )


def body(
    hidden_slab,
    projection,
    adapter_down,
    adapter_up,
    key_gain,
    cache_keys,
    cache_values,
    fresh_keys,
    fresh_values,
    queries,
    slab_length,
    cache_length,
):
    head = lax.axis_index("x")
    y = lax.axis_index("y")
    c = lax.axis_index("c")

    weight_rows = broadcast_over(projection, "z").reshape(80, 2, NX, HD)
    weight_rows = weight_rows.transpose(2, 1, 0, 3).reshape(NX, 160, HD)
    asked = queries.reshape(NX, 8, HD)
    bundle = jnp.concatenate(
        [weight_rows, asked, jnp.zeros((NX, 8, HD), bf16)], axis=1
    )
    bundle = jnp.broadcast_to(bundle[:, None], (NX, NC, 176, HD)).reshape(
        NX * NC, 176, HD
    )
    bundle = lax.all_to_all(bundle, ("x", "c"), 0, 0, tiled=True)
    weight = lax.all_gather(bundle, "y", axis=0, tiled=False)

    def by_head(value):
        return value.reshape(-1, NX, HD).transpose(1, 0, 2)

    count = jnp.broadcast_to(
        cache_length.astype(f32).astype(bf16).reshape(1, 1, 1), (NX, 1, HD)
    )
    context = jnp.concatenate(
        [
            by_head(cache_keys[0]),
            by_head(cache_values[0]),
            by_head(fresh_keys[0]),
            count,
            jnp.zeros((NX, 14, HD), bf16),
            by_head(fresh_values[0]),
            jnp.zeros((NX, 15, HD), bf16),
        ],
        axis=1,
    )
    context = lax.all_to_all(context, "x", 0, 0, tiled=True)
    hidden = broadcast_over(hidden_slab[0], "x")

    up = lax.dynamic_slice(adapter_up[0], (0, 0, head * HD), (2, 32, HD))
    empty = jnp.zeros((32, HD), bf16)
    up = jnp.concatenate(
        [
            jnp.concatenate([up[0], empty], axis=1),
            jnp.concatenate([empty, up[1]], axis=1),
        ],
        axis=0,
    )
    place = jnp.stack([slab_length[0], y, c]).astype(jnp.int32)
    parts = pl.pallas_call(
        rebuild_attend,
        grid=(NX,),
        in_specs=[
            pl.BlockSpec(memory_space=pltpu.SMEM),
            pl.BlockSpec((NY, NC, 176, HD), lambda k: (0, k, 0, 0)),
            pl.BlockSpec((NX, 64, 1280), lambda k: (0, 0, k)),
            pl.BlockSpec((64, 1280), lambda k: (0, k)),
            pl.BlockSpec((64, 256), lambda k: (0, 0)),
            pl.BlockSpec((1, HD), lambda k: (0, 0)),
            pl.BlockSpec((NX, 288, HD), lambda k: (0, 0, 0)),
        ],
        out_specs=pl.BlockSpec((512, 384), lambda k: (0, 0)),
        out_shape=jax.ShapeDtypeStruct((512, 384), bf16),
        scratch_shapes=[
            pltpu.VMEM((256, 256), f32),
            pltpu.VMEM((256, 64), f32),
            pltpu.VMEM((NX, 128, HD), f32),
        ],
        compiler_params=pltpu.CompilerParams(vmem_limit_bytes=48 * 1024 * 1024),
    )(
        place,
        weight,
        hidden,
        adapter_down[0].T,
        up,
        key_gain.reshape(1, HD),
        context,
    )
    parts = lax.all_to_all(parts.reshape(64, 8, 384), CTX, 0, 0, tiled=True)
    slab, attended = pl.pallas_call(
        merge,
        out_shape=[
            jax.ShapeDtypeStruct((64, 1024), bf16),
            jax.ShapeDtypeStruct((32, HD), bf16),
        ],
        compiler_params=pltpu.CompilerParams(vmem_limit_bytes=32 * 1024 * 1024),
    )(parts.reshape(512, 384))
    return slab[None], attended.reshape(1, 1, 32 * HD)


def solution(mesh):
    fine = Mesh(mesh.devices.reshape(NX, NY, NC, NZ), ("x", "y", "c", "z"))
    return jax.shard_map(
        body,
        mesh=fine,
        in_specs=(
            P("z", CTX, None),
            P(CTX + ("z",), None),
            P("z", None, None),
            P("z", None, None, None),
            P(),
            P("z", CTX, None),
            P("z", CTX, None),
            P("z", CTX, None),
            P("z", CTX, None),
            P("z", CTX, None),
            P("z"),
            P("z", CTX),
        ),
        out_specs=(P("z", CTX, None), P("z", CTX, None)),
        check_vma=False,
    )
```

```python
import math

import jax
import jax.numpy as jnp
from jax import lax
from jax.experimental import pallas as pl
from jax.experimental.pallas import tpu as pltpu
from jax.sharding import Mesh, PartitionSpec as P

adapter_scale = 0.5
norm_epsilon = 1e-06
masked_score = -1e30
HD = 128
NX, NY, NC, NZ = 4, 8, 2, 8
HALF = 2560
CTX = ("x", "y", "c")
bf16 = jnp.bfloat16
f32 = jnp.float32


def dot_nt(a, b):
    return lax.dot_general(a, b, (((1,), (1,)), ((), ())), preferred_element_type=f32)


def dot_nn(a, b):
    return lax.dot_general(a, b, (((1,), (0,)), ((), ())), preferred_element_type=f32)


def one_hot(origin, columns):
    lane = lax.broadcasted_iota(jnp.int32, (origin.shape[0], columns), 1)
    return jnp.where(lane == origin, 1.0, 0.0).astype(bf16)


def project(mine, left, right, far_a, far_b, gathered, down, up, keep, send, weight):
    target = lax.broadcasted_iota(jnp.int32, (320, 1), 0)
    s = (target >= 80).astype(jnp.int32)
    s = s + (target >= 160).astype(jnp.int32) + (target >= 240).astype(jnp.int32)
    within = target - 80 * s
    z = (within * 205) >> 11
    pick = one_hot(z * 40 + s * 10 + (within - 10 * z), 320)
    for y in range(NY):
        rows = dot_nn(pick, gathered[y * 320 : (y + 1) * 320, :]).astype(bf16)
        for x in range(2):
            start = x * 1280 + y * 160
            weight[start : start + 160, :] = rows[x * 160 : (x + 1) * 160, :]
    blocks = [mine[...], left[...], right[...]]
    blocks.append(jnp.concatenate([far_a[...], far_b[...]], axis=0))
    for b, rows in enumerate(blocks):
        low = dot_nn(rows, down[...]).astype(bf16)
        part = dot_nn(rows, weight[...]) + adapter_scale * dot_nn(low, up[...])
        keep[b * 64 : (b + 1) * 64, :] = part[0:64, :]
        send[b * 64 : (b + 1) * 64, :] = part[64:128, :].astype(bf16)


def attend(
    place, keep, taken, gain, mine, left, right, far_a, far_b, fresh, *rest
):
    asked, out, ordered = rest[0:NY], rest[NY], rest[NY + 1]
    slab_length = place[0]
    head = place[1]
    y = place[2]
    c = place[3]
    for d in range(NY):
        ordered[(y + NY - d) & 7] = asked[d][...].astype(f32).reshape(NX, 16, HD)
    queries = jnp.stack([ordered[i] for i in range(NY)], axis=1)
    queries = queries.reshape(512, HD).astype(bf16)

    projected = keep[...] + taken[...].astype(f32)
    raw_keys = projected[:, 0:HD]
    mean = jnp.mean(raw_keys * raw_keys, axis=-1, keepdims=True)
    new_keys = (raw_keys * lax.rsqrt(mean + norm_epsilon) * gain[...]).astype(bf16)
    new_values = projected[:, HD:].astype(bf16)

    shards = [head, (head + 3) & 3, (head + 1) & 3, (head + 2) & 3]
    column = lax.broadcasted_iota(jnp.int32, (1, 256), 1)
    block = column >> 6
    source = jnp.where(
        block == 0,
        shards[0],
        jnp.where(block == 1, shards[1], jnp.where(block == 2, shards[2], shards[3])),
    )
    initial = source * 1024 + (y * 2 + c) * 64 + (column & 63)
    slab_scores = jnp.where(
        initial < slab_length, dot_nt(queries, new_keys), masked_score
    )
    key_lanes = pl.ds(pl.multiple_of(head * HD, HD), HD)
    value_lanes = pl.ds(pl.multiple_of(512 + head * HD, HD), HD)
    arrays = [mine, left, right, far_a, far_b]
    cache_keys = jnp.concatenate([a[:, key_lanes] for a in arrays], axis=0)
    cache_values = jnp.concatenate([a[:, value_lanes] for a in arrays], axis=0)
    lane = lax.broadcasted_iota(jnp.int32, (1, HD), 1).astype(f32)
    news = [fresh[2 * shard + c].astype(f32) for shard in shards]
    filled = jnp.concatenate(
        [jnp.where(lane < new[10:11, :], 1.0, 0.0) for new in news], axis=1
    )
    cache_scores = jnp.where(filled > 0.5, dot_nt(queries, cache_keys), masked_score)
    fresh_keys = jnp.concatenate([new[8:9, :] for new in news] * 2, axis=0)
    fresh_values = jnp.concatenate([new[9:10, :] for new in news] * 2, axis=0)
    fresh_keys = fresh_keys.astype(bf16)
    fresh_values = fresh_values.astype(bf16)
    token = lax.broadcasted_iota(jnp.int32, (512, 8), 0) >> 3
    fresh_at = lax.broadcasted_iota(jnp.int32, (1, 8), 1)
    fresh_pos = jnp.where(
        fresh_at == 0,
        shards[0],
        jnp.where(
            fresh_at == 1, shards[1], jnp.where(fresh_at == 2, shards[2], shards[3])
        ),
    )
    fresh_pos = fresh_pos * 16 + y * 2 + c
    fresh_ok = (fresh_at < NX) & (fresh_pos <= token)
    fresh_scores = jnp.where(fresh_ok, dot_nt(queries, fresh_keys), masked_score)

    scale = 1.0 / math.sqrt(HD)
    row_max = jnp.maximum(
        jnp.maximum(
            jnp.max(slab_scores, axis=-1, keepdims=True),
            jnp.max(cache_scores, axis=-1, keepdims=True),
        ),
        jnp.max(fresh_scores, axis=-1, keepdims=True),
    )
    shift = (row_max * scale).astype(bf16).astype(f32)

    def weigh(scores, values):
        weights = jnp.exp(scores * scale - shift).astype(bf16)
        wide = jnp.concatenate([values, jnp.ones_like(values)], axis=1)
        return dot_nn(weights, wide)

    merged = (
        weigh(slab_scores, new_values)
        + weigh(cache_scores, cache_values)
        + weigh(fresh_scores, fresh_values)
    )
    total = merged[:, HD:]
    high = total.astype(bf16).astype(f32)
    lanes = lax.broadcasted_iota(jnp.int32, (512, HD), 1)
    stats = jnp.where(lanes == 0, shift, jnp.where(lanes == 1, high, total - high))
    target = lax.broadcasted_iota(jnp.int32, (512, 1), 0)
    offset = (((target >> 1) & 3) + 4 - head) & 3
    at = jnp.where(
        offset == 0, 0, jnp.where(offset == 1, 2, jnp.where(offset == 2, 3, 1))
    )
    origin = (target & 1) * 256 + at * 64 + (target >> 3)
    spread = dot_nn(
        one_hot(origin, 512), jnp.concatenate([new_keys, new_values], axis=0)
    )
    out[:, 0:HD] = merged[:, 0:HD].astype(bf16)
    out[:, HD : 2 * HD] = stats.astype(bf16)
    out[:, 2 * HD :] = spread.astype(bf16)


def merge(parts, slab, attended):
    heads = []
    rebuilt = []
    for h in range(NX):
        block = parts[h * 128 : (h + 1) * 128, :]
        output = block[:, 0:HD].astype(f32).reshape(16, 8, HD)
        stats = block[:, HD : 2 * HD].astype(f32).reshape(16, 8, HD)
        rebuilt.append(block[:, 2 * HD :])
        shift = stats[:, :, 0:1]
        total = stats[:, :, 1:2] + stats[:, :, 2:3]
        largest = jnp.max(shift, axis=0, keepdims=True)
        factor = jnp.exp(shift - largest)
        merged_total = jnp.sum(factor * total, axis=0)
        merged_output = jnp.sum(factor * output, axis=0)
        heads.append(merged_output / merged_total)
    attended[...] = jnp.concatenate(heads, axis=0).astype(bf16)
    target = lax.broadcasted_iota(jnp.int32, (128, 1), 0)
    origin = (target & 15) * 8 + ((target >> 4) & 3) * 2 + (target >> 6)
    pick = one_hot(origin, 128)
    placed = dot_nn(pick, jnp.concatenate(rebuilt, axis=1)).astype(bf16)
    slab[:, 0:512] = placed[0:64, :]
    slab[:, 512:1024] = placed[64:128, :]


def shift_by(value, axis, step):
    size = lax.axis_size(axis)
    return lax.ppermute(value, axis, [(i, (i + step) % size) for i in range(size)])


def body(
    hidden_slab,
    projection,
    adapter_down,
    adapter_up,
    key_gain,
    cache_keys,
    cache_values,
    fresh_keys,
    fresh_values,
    queries,
    slab_length,
    cache_length,
):
    head = lax.axis_index("x")
    y = lax.axis_index("y")
    c = lax.axis_index("c")

    by_head = projection.reshape(10, 2, NX, HD).transpose(2, 1, 0, 3)
    count = jnp.broadcast_to(
        cache_length.astype(f32).astype(bf16).reshape(1, 1, 1), (NX, 1, HD)
    )
    bundle = jnp.concatenate(
        [
            by_head.reshape(NX, 20, HD),
            queries.reshape(NX, 8, HD),
            fresh_keys.reshape(NX, 1, HD),
            fresh_values.reshape(NX, 1, HD),
            count,
            jnp.zeros((NX, 1, HD), bf16),
        ],
        axis=1,
    )
    bundle = jnp.broadcast_to(bundle[:, None], (NX, NC, 32, HD))
    bundle = lax.all_to_all(
        bundle.reshape(NX * NC, 32, HD), ("x", "c"), 0, 0, tiled=True
    )
    weight = lax.dynamic_slice(bundle, (4 * c, 0, 0), (4, 20, HD))
    weight = weight.reshape(4, 2, 10, HD).transpose(0, 2, 1, 3).reshape(1, 40, 256)
    gathered = lax.all_to_all(
        jnp.broadcast_to(weight, (NY * NZ, 40, 256)), ("y", "z"), 0, 0, tiled=True
    )
    asked = bundle[:, 20:28].reshape(64, HD)
    asked = [asked] + [shift_by(asked, "y", d) for d in range(1, NY)]
    fresh = bundle[:, 20:32]

    rows = hidden_slab[0]
    own = lax.dynamic_slice(rows, (0, c * HALF), (64, HALF))
    other = lax.dynamic_slice(rows, (0, (1 - c) * HALF), (64, HALF))
    other = shift_by(other, "c", 1)
    mine = jnp.concatenate(
        [
            jnp.concatenate([own, other], axis=0),
            cache_keys[0],
            cache_values[0],
        ],
        axis=1,
    )
    left = shift_by(mine, "x", 1)
    right = shift_by(mine, "x", -1)
    far_a = shift_by(left[0:64], "x", 1)
    far_b = shift_by(right[64:128], "x", -1)

    down = lax.dynamic_slice(adapter_down[0], (c * HALF, 0), (HALF, 64))
    up = lax.dynamic_slice(adapter_up[0], (0, 0, head * HD), (2, 32, HD))
    empty = jnp.zeros((32, HD), bf16)
    up = jnp.concatenate(
        [
            jnp.concatenate([up[0], empty], axis=1),
            jnp.concatenate([empty, up[1]], axis=1),
        ],
        axis=0,
    )
    hidden_specs = [pl.BlockSpec((128, HALF), lambda i: (0, 0))] * 3
    hidden_specs += [pl.BlockSpec((64, HALF), lambda i: (0, 0))] * 2
    whole = pl.BlockSpec(memory_space=pltpu.VMEM)
    ring = (mine, left, right, far_a, far_b)
    keep, send = pl.pallas_call(
        project,
        grid=(1,),
        in_specs=hidden_specs + [whole] * 3,
        out_specs=[whole] * 2,
        out_shape=[
            jax.ShapeDtypeStruct((256, 256), f32),
            jax.ShapeDtypeStruct((256, 256), bf16),
        ],
        scratch_shapes=[pltpu.VMEM((HALF, 256), bf16)],
        compiler_params=pltpu.CompilerParams(vmem_limit_bytes=40 * 1024 * 1024),
    )(*ring, gathered.reshape(NY * NZ * 40, 256), down, up)
    taken = shift_by(send, "c", 1)

    place = jnp.stack([slab_length[0], head, y, c]).astype(jnp.int32)
    context = [a[:, HALF:] for a in ring]
    parts = pl.pallas_call(
        attend,
        in_specs=[pl.BlockSpec(memory_space=pltpu.SMEM)] + [whole] * (9 + NY),
        out_specs=whole,
        out_shape=jax.ShapeDtypeStruct((512, 384), bf16),
        scratch_shapes=[pltpu.VMEM((NY, NX, 16, HD), f32)],
        compiler_params=pltpu.CompilerParams(vmem_limit_bytes=40 * 1024 * 1024),
    )(place, keep, taken, key_gain.reshape(1, HD), *context, fresh, *asked)
    parts = lax.all_to_all(parts.reshape(64, 8, 384), CTX, 0, 0, tiled=True)
    slab, attended = pl.pallas_call(
        merge,
        out_shape=[
            jax.ShapeDtypeStruct((64, 1024), bf16),
            jax.ShapeDtypeStruct((32, HD), bf16),
        ],
        compiler_params=pltpu.CompilerParams(vmem_limit_bytes=32 * 1024 * 1024),
    )(parts.reshape(512, 384))
    return slab[None], attended.reshape(1, 1, 32 * HD)


def solution(mesh):
    fine = Mesh(mesh.devices.reshape(NX, NY, NC, NZ), ("x", "y", "c", "z"))
    return jax.shard_map(
        body,
        mesh=fine,
        in_specs=(
            P("z", CTX, None),
            P(CTX + ("z",), None),
            P("z", None, None),
            P("z", None, None, None),
            P(),
            P("z", CTX, None),
            P("z", CTX, None),
            P("z", CTX, None),
            P("z", CTX, None),
            P("z", CTX, None),
            P("z"),
            P("z", CTX),
        ),
        out_specs=(P("z", CTX, None), P("z", CTX, None)),
        check_vma=False,
    )
```

```python
import math

import jax
import jax.numpy as jnp
from jax import lax
from jax.experimental import pallas as pl
from jax.experimental.pallas import tpu as pltpu
from jax.sharding import Mesh, PartitionSpec as P

adapter_scale = 0.5
norm_epsilon = 1e-06
masked_score = -1e30
HD = 128
NX, NY, NC, NZ = 4, 8, 2, 8
HALF = 2560
CTX = ("x", "y", "c")
bf16 = jnp.bfloat16
f32 = jnp.float32


def dot_nt(a, b):
    return lax.dot_general(a, b, (((1,), (1,)), ((), ())), preferred_element_type=f32)


def dot_nn(a, b):
    return lax.dot_general(a, b, (((1,), (0,)), ((), ())), preferred_element_type=f32)


def one_hot(origin, columns):
    lane = lax.broadcasted_iota(jnp.int32, (origin.shape[0], columns), 1)
    return jnp.where(lane == origin, 1.0, 0.0).astype(bf16)


def prepare(weight, asked, new_key, new_value, count, hidden, down, bundle, low):
    filled = jnp.broadcast_to(count[0].astype(f32), (1, HD))
    rows = weight[...].astype(f32)
    questions = asked[...].astype(f32)
    keys = new_key[...].astype(f32)
    values = new_value[...].astype(f32)
    for h in range(NX):
        lanes = slice(h * HD, (h + 1) * HD)
        pieces = [rows[:, lanes], rows[:, 512 + h * HD : 512 + (h + 1) * HD]]
        for g in range(8):
            start = (h * 8 + g) * HD
            pieces.append(questions[:, start : start + HD])
        pieces += [keys[:, lanes], values[:, lanes], filled, jnp.zeros((1, HD), f32)]
        block = jnp.concatenate(pieces, axis=0).astype(bf16)
        bundle[2 * h] = block
        bundle[2 * h + 1] = block
    own = dot_nt(hidden[...], down[...]).astype(bf16)
    low[...] = jnp.concatenate([own, jnp.zeros((64, 64), bf16)], axis=1)


def project(*refs):
    near, other, gathered = refs[0:4], refs[4:8], refs[8]
    keep, send, low = refs[9:12]
    near_rows, other_rows, arrived, weight, sems = refs[12:]
    copies = [pltpu.make_async_copy(gathered, arrived, sems.at[0])]
    for d in range(NX):
        copies.append(pltpu.make_async_copy(near[d], near_rows.at[d], sems.at[1 + d]))
        copies.append(pltpu.make_async_copy(other[d], other_rows.at[d], sems.at[5 + d]))
    for copy in copies:
        copy.start()
    target = lax.broadcasted_iota(jnp.int32, (320, 1), 0)
    s = (target >= 80).astype(jnp.int32)
    s = s + (target >= 160).astype(jnp.int32) + (target >= 240).astype(jnp.int32)
    within = target - 80 * s
    z = (within * 205) >> 11
    pick = one_hot(z * 40 + s * 10 + (within - 10 * z), 320)
    copies[0].wait()
    for y in range(NY):
        rows = dot_nn(pick, arrived[y * 320 : (y + 1) * 320, :]).astype(bf16)
        for x in range(2):
            start = x * 1280 + y * 160
            weight[start : start + 160, :] = rows[x * 160 : (x + 1) * 160, :]
    for copy in copies[1:]:
        copy.wait()
    for d in range(NX):
        low[d * 64 : (d + 1) * 64, :] = near_rows[d, :, HALF:]
    keep[...] = dot_nn(near_rows[:, :, 0:HALF].reshape(256, HALF), weight[...])
    send[...] = dot_nn(other_rows[...].reshape(256, HALF), weight[...])


def attend(place, keep, taken, low, up, gain, *rest):
    context, fresh, asked = rest[0:NX], rest[NX], rest[NX + 1 : NX + 5]
    out, ordered = rest[NX + 5 :]
    slab_length = place[0]
    head = place[1]
    y = place[2]
    c = place[3]
    for d in range(NY):
        part, row = [(0, 0), (1, 0), (2, 0), (2, 1), (3, 0), (3, 1), (3, 2), (3, 3)][d]
        block = asked[part][row * 64 : (row + 1) * 64, :]
        ordered[(y + NY - d) & 7] = block.astype(f32).reshape(NX, 16, HD)
    queries = jnp.stack([ordered[i] for i in range(NY)], axis=1)
    queries = queries.reshape(512, HD).astype(bf16)

    delta = dot_nn(low[:, 0:64], up[...])
    projected = keep[...] + taken[...] + adapter_scale * delta
    raw_keys = projected[:, 0:HD]
    mean = jnp.mean(raw_keys * raw_keys, axis=-1, keepdims=True)
    new_keys = (raw_keys * lax.rsqrt(mean + norm_epsilon) * gain[...]).astype(bf16)
    new_values = projected[:, HD:].astype(bf16)

    shards = [(head + NX - d) & 3 for d in range(NX)]

    def by_block(index):
        return jnp.where(
            index == 0,
            shards[0],
            jnp.where(index == 1, shards[1], jnp.where(index == 2, shards[2], shards[3])),
        )

    column = lax.broadcasted_iota(jnp.int32, (1, 256), 1)
    initial = by_block(column >> 6) * 1024 + (y * 2 + c) * 64 + (column & 63)
    slab_scores = jnp.where(
        initial < slab_length, dot_nt(queries, new_keys), masked_score
    )
    cache_keys = jnp.concatenate([a[0:128, :] for a in context], axis=0)
    cache_values = jnp.concatenate([a[128:256, :] for a in context], axis=0)
    lane = lax.broadcasted_iota(jnp.int32, (1, HD), 1).astype(f32)
    news = [fresh[2 * shard + c].astype(f32) for shard in shards]
    filled = jnp.concatenate(
        [jnp.where(lane < new[10:11, :], 1.0, 0.0) for new in news], axis=1
    )
    cache_scores = jnp.where(filled > 0.5, dot_nt(queries, cache_keys), masked_score)
    fresh_keys = jnp.concatenate([new[8:9, :] for new in news] * 2, axis=0)
    fresh_values = jnp.concatenate([new[9:10, :] for new in news] * 2, axis=0)
    fresh_keys = fresh_keys.astype(bf16)
    fresh_values = fresh_values.astype(bf16)
    token = lax.broadcasted_iota(jnp.int32, (512, 8), 0) >> 3
    fresh_at = lax.broadcasted_iota(jnp.int32, (1, 8), 1)
    fresh_pos = by_block(fresh_at) * 16 + y * 2 + c
    fresh_ok = (fresh_at < NX) & (fresh_pos <= token)
    fresh_scores = jnp.where(fresh_ok, dot_nt(queries, fresh_keys), masked_score)

    scale = 1.0 / math.sqrt(HD)
    row_max = jnp.maximum(
        jnp.maximum(
            jnp.max(slab_scores, axis=-1, keepdims=True),
            jnp.max(cache_scores, axis=-1, keepdims=True),
        ),
        jnp.max(fresh_scores, axis=-1, keepdims=True),
    )
    shift = (row_max * scale).astype(bf16).astype(f32)

    def weigh(scores, values):
        weights = jnp.exp(scores * scale - shift).astype(bf16)
        wide = jnp.concatenate([values, jnp.ones_like(values)], axis=1)
        return dot_nn(weights, wide)

    merged = (
        weigh(slab_scores, new_values)
        + weigh(cache_scores, cache_values)
        + weigh(fresh_scores, fresh_values)
    )
    total = merged[:, HD:]
    high = total.astype(bf16).astype(f32)
    lanes = lax.broadcasted_iota(jnp.int32, (512, HD), 1)
    stats = jnp.where(lanes == 0, shift, jnp.where(lanes == 1, high, total - high))
    target = lax.broadcasted_iota(jnp.int32, (512, 1), 0)
    at = (head + NX - ((target >> 1) & 3)) & 3
    origin = (target & 1) * 256 + at * 64 + (target >> 3)
    spread = dot_nn(
        one_hot(origin, 512), jnp.concatenate([new_keys, new_values], axis=0)
    )
    out[:, 0:HD] = merged[:, 0:HD].astype(bf16)
    out[:, HD : 2 * HD] = stats.astype(bf16)
    out[:, 2 * HD :] = spread.astype(bf16)


def merge(parts, slab, attended):
    heads = []
    rebuilt = []
    for h in range(NX):
        block = parts[h * 128 : (h + 1) * 128, :]
        output = block[:, 0:HD].astype(f32).reshape(16, 8, HD)
        stats = block[:, HD : 2 * HD].astype(f32).reshape(16, 8, HD)
        rebuilt.append(block[:, 2 * HD :])
        shift = stats[:, :, 0:1]
        total = stats[:, :, 1:2] + stats[:, :, 2:3]
        largest = jnp.max(shift, axis=0, keepdims=True)
        factor = jnp.exp(shift - largest)
        merged_total = jnp.sum(factor * total, axis=0)
        merged_output = jnp.sum(factor * output, axis=0)
        heads.append(merged_output / merged_total)
    for h in range(NX):
        for g in range(8):
            start = (h * 8 + g) * HD
            attended[:, start : start + HD] = heads[h][g : g + 1, :].astype(bf16)
    target = lax.broadcasted_iota(jnp.int32, (128, 1), 0)
    origin = (target & 15) * 8 + ((target >> 4) & 3) * 2 + (target >> 6)
    pick = one_hot(origin, 128)
    placed = dot_nn(pick, jnp.concatenate(rebuilt, axis=1)).astype(bf16)
    slab[:, 0:512] = placed[0:64, :]
    slab[:, 512:1024] = placed[64:128, :]


def shift_by(value, axis, step):
    size = lax.axis_size(axis)
    return lax.ppermute(value, axis, [(i, (i + step) % size) for i in range(size)])


def body(
    hidden_slab,
    projection,
    adapter_down,
    adapter_up,
    key_gain,
    cache_keys,
    cache_values,
    fresh_keys,
    fresh_values,
    queries,
    slab_length,
    cache_length,
):
    head = lax.axis_index("x")
    y = lax.axis_index("y")
    c = lax.axis_index("c")
    whole = pl.BlockSpec(memory_space=pltpu.VMEM)
    scalars = pl.BlockSpec(memory_space=pltpu.SMEM)
    anywhere = pl.BlockSpec(memory_space=pl.ANY)
    rows = hidden_slab[0]

    bundle, low = pl.pallas_call(
        prepare,
        in_specs=[whole] * 4 + [scalars] + [whole] * 2,
        out_specs=[whole] * 2,
        out_shape=[
            jax.ShapeDtypeStruct((NX * NC, 32, HD), bf16),
            jax.ShapeDtypeStruct((64, HD), bf16),
        ],
        compiler_params=pltpu.CompilerParams(vmem_limit_bytes=24 * 1024 * 1024),
    )(
        projection,
        queries[0],
        fresh_keys[0],
        fresh_values[0],
        cache_length[0],
        rows,
        adapter_down[0].T,
    )
    bundle = lax.all_to_all(bundle, ("x", "c"), 0, 0, tiled=True)
    weight = lax.dynamic_slice(bundle, (4 * c, 0, 0), (4, 20, HD))
    weight = weight.reshape(4, 2, 10, HD).transpose(0, 2, 1, 3).reshape(1, 40, 256)
    gathered = lax.all_to_all(
        jnp.broadcast_to(weight, (NY * NZ, 40, 256)), ("y", "z"), 0, 0, tiled=True
    )
    asked = [bundle[:, 20:28].reshape(64, HD)]
    asked.append(shift_by(asked[0], "y", 1))
    asked.append(shift_by(jnp.concatenate(asked, axis=0), "y", 2))
    asked.append(shift_by(jnp.concatenate(asked, axis=0), "y", 4))
    fresh = bundle[:, 20:32]

    own = lax.dynamic_slice(rows, (0, c * HALF), (64, HALF))
    own = jnp.concatenate([own, low], axis=1)
    other = lax.dynamic_slice(rows, (0, (1 - c) * HALF), (64, HALF))
    other = shift_by(other, "c", 1)
    near = [own, shift_by(own, "x", 1), None, shift_by(own, "x", -1)]
    others = [other, shift_by(other, "x", 1), None, shift_by(other, "x", -1)]
    near[2] = shift_by(near[1], "x", 1)
    others[2] = shift_by(others[3], "x", -1)

    by_head = jnp.concatenate([cache_keys[0], cache_values[0]], axis=0)
    by_head = by_head.reshape(256, NX, HD).transpose(1, 0, 2)
    context = []
    for d in range(NX):
        block = lax.dynamic_index_in_dim(by_head, (head + d) & 3, 0, keepdims=False)
        context.append(block if d == 0 else shift_by(block, "x", d))

    up = lax.dynamic_slice(adapter_up[0], (0, 0, head * HD), (2, 32, HD))
    empty = jnp.zeros((32, HD), bf16)
    up = jnp.concatenate(
        [
            jnp.concatenate([up[0], empty], axis=1),
            jnp.concatenate([empty, up[1]], axis=1),
        ],
        axis=0,
    )
    gathered, asked, context, up, fresh = lax.optimization_barrier(
        (gathered, asked, context, up, fresh)
    )
    keep, send, low = pl.pallas_call(
        project,
        in_specs=[anywhere] * 9,
        out_specs=[whole] * 3,
        out_shape=[
            jax.ShapeDtypeStruct((256, 256), f32),
            jax.ShapeDtypeStruct((256, 256), f32),
            jax.ShapeDtypeStruct((256, HD), bf16),
        ],
        scratch_shapes=[
            pltpu.VMEM((NX, 64, HALF + HD), bf16),
            pltpu.VMEM((NX, 64, HALF), bf16),
            pltpu.VMEM((HALF, 256), bf16),
            pltpu.VMEM((HALF, 256), bf16),
            pltpu.SemaphoreType.DMA((9,)),
        ],
        compiler_params=pltpu.CompilerParams(vmem_limit_bytes=32 * 1024 * 1024),
    )(*near, *others, gathered.reshape(HALF, 256))
    taken = shift_by(send, "c", 1)

    place = jnp.stack([slab_length[0], head, y, c]).astype(jnp.int32)
    parts = pl.pallas_call(
        attend,
        in_specs=[scalars] + [whole] * 14,
        out_specs=whole,
        out_shape=jax.ShapeDtypeStruct((512, 384), bf16),
        scratch_shapes=[pltpu.VMEM((NY, NX, 16, HD), f32)],
        compiler_params=pltpu.CompilerParams(vmem_limit_bytes=32 * 1024 * 1024),
    )(place, keep, taken, low, up, key_gain.reshape(1, HD), *context, fresh, *asked)
    parts = lax.all_to_all(parts.reshape(64, 8, 384), CTX, 0, 0, tiled=True)
    slab, attended = pl.pallas_call(
        merge,
        out_shape=[
            jax.ShapeDtypeStruct((64, 1024), bf16),
            jax.ShapeDtypeStruct((1, 32 * HD), bf16),
        ],
        compiler_params=pltpu.CompilerParams(vmem_limit_bytes=24 * 1024 * 1024),
    )(parts.reshape(512, 384))
    return slab[None], attended[None]


def solution(mesh):
    fine = Mesh(mesh.devices.reshape(NX, NY, NC, NZ), ("x", "y", "c", "z"))
    return jax.shard_map(
        body,
        mesh=fine,
        in_specs=(
            P("z", CTX, None),
            P(CTX + ("z",), None),
            P("z", None, None),
            P("z", None, None, None),
            P(),
            P("z", CTX, None),
            P("z", CTX, None),
            P("z", CTX, None),
            P("z", CTX, None),
            P("z", CTX, None),
            P("z"),
            P("z", CTX),
        ),
        out_specs=(P("z", CTX, None), P("z", CTX, None)),
        check_vma=False,
    )
```

```python
import math

import jax
import jax.numpy as jnp
from jax import lax
from jax.experimental import pallas as pl
from jax.experimental.pallas import tpu as pltpu
from jax.sharding import Mesh, PartitionSpec as P

adapter_scale = 0.5
norm_epsilon = 1e-06
masked_score = -1e30
HD = 128
score_scale = 1.0 / math.sqrt(HD)
NX, NY, NC, NZ = 4, 8, 2, 8
HALF = 2560
CTX = ("x", "y", "c")
bf16 = jnp.bfloat16
f32 = jnp.float32


def dot_nt(a, b):
    return lax.dot_general(a, b, (((1,), (1,)), ((), ())), preferred_element_type=f32)


def dot_nn(a, b):
    return lax.dot_general(a, b, (((1,), (0,)), ((), ())), preferred_element_type=f32)


def one_hot(origin, columns):
    lane = lax.broadcasted_iota(jnp.int32, (origin.shape[0], columns), 1)
    return jnp.where(lane == origin, 1.0, 0.0).astype(bf16)


def fetch(pairs, sems):
    copies = [
        pltpu.make_async_copy(source, target, sems.at[i])
        for i, (source, target) in enumerate(pairs)
    ]
    for copy in copies:
        copy.start()
    return copies


def bundle_up(*refs):
    inputs, lengths, bundle, held, sems = refs[0:6], refs[6], refs[7], refs[8:14], refs[14]
    copies = fetch(list(zip(inputs, held)), sems)
    for copy in copies:
        copy.wait()
    weight, asked, new_key, new_value, keys, values = [ref[...] for ref in held]
    filled = jnp.broadcast_to(lengths[0].astype(f32), (1, HD))
    lane = lax.broadcasted_iota(jnp.int32, (1, HD), 1)
    live = jnp.where(lane < 64, lengths[1] >> 6, lengths[1] & 63).astype(f32)
    rows = weight.astype(f32)
    small = [ref.astype(f32) for ref in (new_key, new_value, asked)]
    for h in range(NX):
        lanes = slice(h * HD, (h + 1) * HD)
        pieces = [rows[:, lanes], rows[:, 512 + h * HD : 512 + (h + 1) * HD]]
        pieces += [small[0][:, lanes], small[1][:, lanes]]
        pieces += [filled, live]
        for g in range(8):
            start = (h * 8 + g) * HD
            pieces.append(small[2][:, start : start + HD])
        bundle[h, 0:32, :] = jnp.concatenate(pieces, axis=0).astype(bf16)
        bundle[h, 32:160, :] = keys[:, lanes]
        bundle[h, 160:288, :] = values[:, lanes]


def project(*refs):
    blocks, gathered, other, down_in, up_in, out = refs[0:5], *refs[5:10]
    rows, arrived, weight, down, up, sems = refs[10:]
    c = lax.axis_index("c")
    head = lax.axis_index("x")
    up_in = up_in.at[:, :, pl.ds(pl.multiple_of(head * HD, HD), HD)]
    pairs = [(gathered, arrived.at[0]), (other, arrived.at[1])]
    pairs += [(down_in, down), (up_in, up)]
    start = 0
    for block in blocks:
        size = block.shape[0]
        pairs.append((block, rows.at[start : start + size, :]))
        start += size
    copies = fetch(pairs, sems)
    target = lax.broadcasted_iota(jnp.int32, (320, 1), 0)
    x = (target >= 80).astype(jnp.int32)
    x = x + (target >= 160).astype(jnp.int32) + (target >= 240).astype(jnp.int32)
    within = target - 80 * x
    z = (within * 205) >> 11
    pick = one_hot(z * 40 + x * 10 + (within - 10 * z), 320)
    for side in range(NC):
        core = c if side == 0 else 1 - c
        copies[side].wait()
        for y in range(NY):
            block = arrived[side, y * 320 : (y + 1) * 320, :]
            picked = dot_nn(pick, block).astype(bf16)
            for x in range(NX):
                weight[x, y, core] = picked[x * 80 : (x + 1) * 80]
    for copy in copies[2:]:
        copy.wait()
    low = dot_nt(rows[...], down[...]).astype(bf16)
    base = dot_nn(rows[...], weight[...].reshape(2 * HALF, 256))
    out[:, 0:HD] = base[:, 0:HD] + adapter_scale * dot_nn(low[:, 0:32], up[0])
    out[:, HD:] = base[:, HD:] + adapter_scale * dot_nn(low[:, 32:64], up[1])


def attend(*refs):
    inputs, out, held, sems = refs[0:4], refs[4], refs[5:9], refs[9]
    copies = fetch(list(zip(inputs, held)), sems)
    asked, bundle, projected, gain = held
    head = lax.axis_index("x")
    y = lax.axis_index("y")
    c = lax.axis_index("c")
    copies[0].wait()
    queries = asked[...].astype(f32).reshape(NY * NC, NX, 8, HD)
    queries = jnp.stack([queries[:, i] for i in range(NX)], axis=0)
    queries = queries.reshape(512, HD).astype(bf16)

    copies[1].wait()
    cache_keys = bundle[:, 32:160, :].reshape(512, HD)
    cache_values = bundle[:, 160:288, :].reshape(512, HD)
    lane = lax.broadcasted_iota(jnp.int32, (1, HD), 1).astype(f32)
    news = [bundle[i, 16:32, :].astype(f32) for i in range(NX)]
    filled = jnp.concatenate(
        [jnp.where(lane < new[6:7, :], 1.0, 0.0) for new in news], axis=1
    )
    cache_scores = jnp.where(filled > 0.5, dot_nt(queries, cache_keys), masked_score)
    fresh_keys = jnp.concatenate([new[4:5, :] for new in news] * 2, axis=0)
    fresh_values = jnp.concatenate([new[5:6, :] for new in news] * 2, axis=0)
    fresh_keys = fresh_keys.astype(bf16)
    fresh_values = fresh_values.astype(bf16)
    token = lax.broadcasted_iota(jnp.int32, (512, 8), 0) >> 3
    fresh_at = lax.broadcasted_iota(jnp.int32, (1, 8), 1)
    fresh_ok = (fresh_at < NX) & (fresh_at * 16 + y * 2 + c <= token)
    fresh_scores = jnp.where(fresh_ok, dot_nt(queries, fresh_keys), masked_score)

    copies[2].wait()
    copies[3].wait()
    raw_keys = projected[:, 0:HD]
    mean = jnp.mean(raw_keys * raw_keys, axis=-1, keepdims=True)
    new_keys = (raw_keys * lax.rsqrt(mean + norm_epsilon) * gain[...]).astype(bf16)
    new_values = projected[:, HD:].astype(bf16)
    column = lax.broadcasted_iota(jnp.int32, (1, 256), 1)
    shard = (head + NX - (column >> 6)) & 3
    initial = shard * 1024 + (y * 2 + c) * 64 + (column & 63)
    slab_length = news[0][7:8, 0:1] * 64.0 + news[0][7:8, 64:65]
    live = initial.astype(f32) < slab_length
    slab_scores = jnp.where(
        live, dot_nt(queries, new_keys), masked_score
    )

    row_max = jnp.maximum(
        jnp.maximum(
            jnp.max(slab_scores, axis=-1, keepdims=True),
            jnp.max(cache_scores, axis=-1, keepdims=True),
        ),
        jnp.max(fresh_scores, axis=-1, keepdims=True),
    )
    shift = (row_max * score_scale).astype(bf16).astype(f32)

    def weigh(scores, values):
        weights = jnp.exp(scores * score_scale - shift).astype(bf16)
        wide = jnp.concatenate([values, jnp.ones_like(values)], axis=1)
        return dot_nn(weights, wide)

    merged = (
        weigh(slab_scores, new_values)
        + weigh(cache_scores, cache_values)
        + weigh(fresh_scores, fresh_values)
    )
    total = merged[:, HD:]
    high = total.astype(bf16).astype(f32)
    lanes = lax.broadcasted_iota(jnp.int32, (512, HD), 1)
    stats = jnp.where(lanes == 0, shift, jnp.where(lanes == 1, high, total - high))
    target = lax.broadcasted_iota(jnp.int32, (512, 1), 0)
    at = (head + NX - ((target >> 1) & 3)) & 3
    origin = (target & 1) * 256 + at * 64 + (target >> 3)
    spread = dot_nn(
        one_hot(origin, 512), jnp.concatenate([new_keys, new_values], axis=0)
    )
    out[:, 0:HD] = merged[:, 0:HD].astype(bf16)
    out[:, HD : 2 * HD] = stats.astype(bf16)
    out[:, 2 * HD :] = spread.astype(bf16)


def merge(parts, slab, attended):
    heads = []
    rebuilt = []
    for h in range(NX):
        block = parts[h * 128 : (h + 1) * 128, :]
        output = block[:, 0:HD].astype(f32).reshape(16, 8, HD)
        stats = block[:, HD : 2 * HD].astype(f32).reshape(16, 8, HD)
        rebuilt.append(block[:, 2 * HD :])
        shift = stats[:, :, 0:1]
        total = stats[:, :, 1:2] + stats[:, :, 2:3]
        largest = jnp.max(shift, axis=0, keepdims=True)
        factor = jnp.exp(shift - largest)
        merged_total = jnp.sum(factor * total, axis=0)
        merged_output = jnp.sum(factor * output, axis=0)
        heads.append(merged_output / merged_total)
    for h in range(NX):
        for g in range(8):
            start = (h * 8 + g) * HD
            attended[:, start : start + HD] = heads[h][g : g + 1, :].astype(bf16)
    target = lax.broadcasted_iota(jnp.int32, (128, 1), 0)
    origin = (target & 15) * 8 + ((target >> 4) & 3) * 2 + (target >> 6)
    pick = one_hot(origin, 128)
    placed = dot_nn(pick, jnp.concatenate(rebuilt, axis=1)).astype(bf16)
    slab[:, 0:512] = placed[0:64, :]
    slab[:, 512:1024] = placed[64:128, :]


def shift_by(value, axis, step):
    size = lax.axis_size(axis)
    return lax.ppermute(value, axis, [(i, (i + step) % size) for i in range(size)])


def body(
    hidden_slab,
    projection,
    adapter_down,
    adapter_up,
    key_gain,
    cache_keys,
    cache_values,
    fresh_keys,
    fresh_values,
    queries,
    slab_length,
    cache_length,
):
    c = lax.axis_index("c")
    whole = pl.BlockSpec(memory_space=pltpu.VMEM)
    scalars = pl.BlockSpec(memory_space=pltpu.SMEM)
    anywhere = pl.BlockSpec(memory_space=pl.ANY)
    rows = hidden_slab[0]

    inputs = [projection, queries[0], fresh_keys[0], fresh_values[0]]
    inputs += [cache_keys[0], cache_values[0]]
    bundle = pl.pallas_call(
        bundle_up,
        in_specs=[anywhere] * 6 + [scalars],
        out_specs=whole,
        out_shape=jax.ShapeDtypeStruct((NX, 288, HD), bf16),
        scratch_shapes=[pltpu.VMEM(a.shape, bf16) for a in inputs]
        + [pltpu.SemaphoreType.DMA((6,))],
        compiler_params=pltpu.CompilerParams(vmem_limit_bytes=56 * 1024 * 1024),
    )(*inputs, jnp.concatenate([cache_length[0], slab_length]))
    bundle = lax.all_to_all(bundle, "x", 0, 0, tiled=True)

    weight = bundle[:, 0:20].reshape(NX, 2, 10, HD)
    weight = weight.transpose(0, 2, 1, 3).reshape(1, 40, 256)
    gathered = lax.all_to_all(
        jnp.broadcast_to(weight, (NY * NZ, 40, 256)), ("y", "z"), 0, 0, tiled=True
    )
    left = shift_by(rows, "x", 1)
    right = shift_by(rows, "x", -1)
    far_a = shift_by(left[0:32], "x", 1)
    far_b = shift_by(right[32:64], "x", -1)
    asked = bundle[:, 24:32].reshape(1, 32, HD)
    asked = jnp.broadcast_to(asked, (NY * NC, 32, HD))

    gathered, asked, far_a, far_b = lax.optimization_barrier(
        (gathered.reshape(HALF, 256), asked, far_a, far_b)
    )
    other = shift_by(gathered, "c", 1)
    asked = lax.all_to_all(asked, ("y", "c"), 0, 0, tiled=True)
    projected = pl.pallas_call(
        project,
        in_specs=[anywhere] * 9,
        out_specs=whole,
        out_shape=jax.ShapeDtypeStruct((256, 256), f32),
        scratch_shapes=[
            pltpu.VMEM((256, 2 * HALF), bf16),
            pltpu.VMEM((NC, HALF, 256), bf16),
            pltpu.VMEM((NX, NY, NC, 80, 256), bf16),
            pltpu.VMEM((64, 2 * HALF), bf16),
            pltpu.VMEM((2, 32, HD), bf16),
            pltpu.SemaphoreType.DMA((9,)),
        ],
        compiler_params=pltpu.CompilerParams(vmem_limit_bytes=56 * 1024 * 1024),
        cost_estimate=pl.CostEstimate(
            flops=1400000000, bytes_accessed=8000000, transcendentals=0
        ),
    )(
        rows,
        left,
        far_a,
        far_b,
        right,
        gathered,
        other,
        adapter_down[0].T,
        adapter_up[0],
    )

    parts = pl.pallas_call(
        attend,
        in_specs=[anywhere] * 4,
        out_specs=whole,
        out_shape=jax.ShapeDtypeStruct((512, 384), bf16),
        scratch_shapes=[
            pltpu.VMEM((NY * NC, 32, HD), bf16),
            pltpu.VMEM((NX, 288, HD), bf16),
            pltpu.VMEM((256, 256), f32),
            pltpu.VMEM((1, HD), f32),
            pltpu.SemaphoreType.DMA((4,)),
        ],
        compiler_params=pltpu.CompilerParams(vmem_limit_bytes=56 * 1024 * 1024),
    )(asked, bundle, projected, key_gain.reshape(1, HD))
    parts = lax.all_to_all(parts.reshape(64, 8, 384), CTX, 0, 0, tiled=True)
    slab, attended = pl.pallas_call(
        merge,
        out_shape=[
            jax.ShapeDtypeStruct((64, 1024), bf16),
            jax.ShapeDtypeStruct((1, 32 * HD), bf16),
        ],
        compiler_params=pltpu.CompilerParams(vmem_limit_bytes=24 * 1024 * 1024),
    )(parts.reshape(512, 384))
    return slab[None], attended[None]


def solution(mesh):
    fine = Mesh(mesh.devices.reshape(NX, NY, NC, NZ), ("x", "y", "c", "z"))
    return jax.shard_map(
        body,
        mesh=fine,
        in_specs=(
            P("z", CTX, None),
            P(CTX + ("z",), None),
            P("z", None, None),
            P("z", None, None, None),
            P(),
            P("z", CTX, None),
            P("z", CTX, None),
            P("z", CTX, None),
            P("z", CTX, None),
            P("z", CTX, None),
            P("z"),
            P("z", CTX),
        ),
        out_specs=(P("z", CTX, None), P("z", CTX, None)),
        check_vma=False,
    )
```

```python
import math

import jax
import jax.numpy as jnp
from jax import lax
from jax.experimental import pallas as pl
from jax.experimental.pallas import tpu as pltpu
from jax.sharding import Mesh, PartitionSpec as P

adapter_scale = 0.5
norm_epsilon = 1e-06
masked_score = -1e30
HD = 128
score_scale = 1.0 / math.sqrt(HD)
NX, NY, NC, NZ = 4, 8, 2, 8
HALF = 2560
CTX = ("x", "y", "c")
bf16 = jnp.bfloat16
f32 = jnp.float32


def dot_nt(a, b):
    return lax.dot_general(a, b, (((1,), (1,)), ((), ())), preferred_element_type=f32)


def dot_nn(a, b):
    return lax.dot_general(a, b, (((1,), (0,)), ((), ())), preferred_element_type=f32)


def one_hot(origin, columns):
    lane = lax.broadcasted_iota(jnp.int32, (origin.shape[0], columns), 1)
    return jnp.where(lane == origin, 1.0, 0.0).astype(bf16)


def fetch(pairs, sems):
    copies = [
        pltpu.make_async_copy(source, target, sems.at[i])
        for i, (source, target) in enumerate(pairs)
    ]
    for copy in copies:
        copy.start()
    return copies


def bundle_up(*refs):
    inputs, bundle, held, sems = refs[0:8], refs[8], refs[9:17], refs[17]
    copies = fetch(list(zip(inputs, held)), sems)
    for copy in copies:
        copy.wait()
    weight, asked, new_key, new_value, keys, values, count, length = [
        ref[...] for ref in held
    ]
    filled = jnp.broadcast_to(count.astype(f32), (1, HD))
    lane = lax.broadcasted_iota(jnp.int32, (1, HD), 1)
    live = jnp.where(lane < 64, length >> 6, length & 63).astype(f32)
    rows = weight.astype(f32)
    small = [ref.astype(f32) for ref in (new_key, new_value, asked)]
    for h in range(NX):
        lanes = slice(h * HD, (h + 1) * HD)
        pieces = [rows[:, lanes], rows[:, 512 + h * HD : 512 + (h + 1) * HD]]
        pieces += [small[0][:, lanes], small[1][:, lanes]]
        pieces += [filled, live]
        for g in range(8):
            start = (h * 8 + g) * HD
            pieces.append(small[2][:, start : start + HD])
        bundle[h, 0:32, :] = jnp.concatenate(pieces, axis=0).astype(bf16)
        bundle[h, 32:160, :] = keys[:, lanes]
        bundle[h, 160:288, :] = values[:, lanes]


def fan_out(bundle, weight, asked, held, sems):
    copy = pltpu.make_async_copy(bundle.at[:, 0:32, :], held, sems.at[0])
    copy.start()
    copy.wait()
    rows = [held[x].astype(f32) for x in range(NX)]
    block = jnp.concatenate([jnp.concatenate([a[0:10], a[10:20]], axis=1) for a in rows])
    block = block.astype(bf16)
    for i in range(NY * NZ):
        weight[i] = block
    block = jnp.concatenate([a[24:32] for a in rows], axis=0).astype(bf16)
    for i in range(NY * NC):
        asked[i] = block


def project(*refs):
    blocks, gathered, other, down_in, up_in, gain_in, out = refs[0:5], *refs[5:11]
    rows, arrived, weight, down, up, gain, sems = refs[11:]
    c = lax.axis_index("c")
    head = lax.axis_index("x")
    up_in = up_in.at[:, :, pl.ds(pl.multiple_of(head * HD, HD), HD)]
    pairs = [(gathered, arrived.at[0]), (other, arrived.at[1])]
    pairs += [(down_in, down), (up_in, up), (gain_in, gain)]
    start = 0
    for block in blocks:
        size = block.shape[0]
        pairs.append((block, rows.at[start : start + size, :]))
        start += size
    copies = fetch(pairs, sems)
    target = lax.broadcasted_iota(jnp.int32, (160, 1), 0)
    x = (target >= 40).astype(jnp.int32)
    x = x + (target >= 80).astype(jnp.int32) + (target >= 120).astype(jnp.int32)
    within = target - 40 * x
    z = (within * 205) >> 11
    pick = one_hot(z * 40 + x * 10 + (within - 10 * z), 160)
    target = lax.broadcasted_iota(jnp.int32, (512, 1), 0)
    at = (head + NX - ((target >> 1) & 3)) & 3
    spread = one_hot((target & 1) * 256 + at * 64 + (target >> 3), 512)
    for side in range(NC):
        core = c if side == 0 else 1 - c
        copies[side].wait()
        for y in range(NY):
            picked = []
            for half in range(2):
                start = y * 320 + half * 160
                picked.append(dot_nn(pick, arrived[side, start : start + 160, :]))
            for x in range(NX):
                own = [a[x * 40 : (x + 1) * 40] for a in picked]
                weight[x, y, core] = jnp.concatenate(own, axis=0).astype(bf16)
    for copy in copies[2:]:
        copy.wait()
    low = dot_nt(rows[...], down[...]).astype(bf16)
    base = dot_nn(rows[...], weight[...].reshape(2 * HALF, 256))
    raw_keys = base[:, 0:HD] + adapter_scale * dot_nn(low[:, 0:32], up[0])
    new_values = base[:, HD:] + adapter_scale * dot_nn(low[:, 32:64], up[1])
    mean = jnp.mean(raw_keys * raw_keys, axis=-1, keepdims=True)
    new_keys = raw_keys * lax.rsqrt(mean + norm_epsilon) * gain[...]
    rebuilt = jnp.concatenate([new_keys, new_values], axis=0).astype(bf16)
    out[:, 0:HD] = rebuilt
    out[:, HD:] = dot_nn(spread, rebuilt).astype(bf16)


def attend(*refs):
    inputs, out, held, sems = refs[0:3], refs[3], refs[4:7], refs[7]
    copies = fetch(list(zip(inputs, held)), sems)
    asked, bundle, rebuilt = held
    head = lax.axis_index("x")
    y = lax.axis_index("y")
    c = lax.axis_index("c")
    copies[0].wait()
    queries = asked[...].astype(f32).reshape(NY * NC, NX, 8, HD)
    queries = jnp.stack([queries[:, i] for i in range(NX)], axis=0)
    queries = queries.reshape(512, HD).astype(bf16)

    copies[1].wait()
    cache_keys = bundle[:, 32:160, :].reshape(512, HD)
    cache_values = bundle[:, 160:288, :].reshape(512, HD)
    lane = lax.broadcasted_iota(jnp.int32, (1, HD), 1).astype(f32)
    news = [bundle[i, 16:32, :].astype(f32) for i in range(NX)]
    filled = jnp.concatenate(
        [jnp.where(lane < new[6:7, :], 1.0, 0.0) for new in news], axis=1
    )
    cache_scores = jnp.where(filled > 0.5, dot_nt(queries, cache_keys), masked_score)
    fresh_keys = jnp.concatenate([new[4:5, :] for new in news] * 2, axis=0)
    fresh_values = jnp.concatenate([new[5:6, :] for new in news] * 2, axis=0)
    fresh_keys = fresh_keys.astype(bf16)
    fresh_values = fresh_values.astype(bf16)
    token = lax.broadcasted_iota(jnp.int32, (512, 8), 0) >> 3
    fresh_at = lax.broadcasted_iota(jnp.int32, (1, 8), 1)
    fresh_ok = (fresh_at < NX) & (fresh_at * 16 + y * 2 + c <= token)
    fresh_scores = jnp.where(fresh_ok, dot_nt(queries, fresh_keys), masked_score)

    copies[2].wait()
    new_keys = rebuilt[0:256, 0:HD]
    new_values = rebuilt[256:512, 0:HD]
    column = lax.broadcasted_iota(jnp.int32, (1, 256), 1)
    shard = (head + NX - (column >> 6)) & 3
    initial = shard * 1024 + (y * 2 + c) * 64 + (column & 63)
    slab_length = news[0][7:8, 0:1] * 64.0 + news[0][7:8, 64:65]
    live = initial.astype(f32) < slab_length
    slab_scores = jnp.where(
        live, dot_nt(queries, new_keys), masked_score
    )

    row_max = jnp.maximum(
        jnp.maximum(
            jnp.max(slab_scores, axis=-1, keepdims=True),
            jnp.max(cache_scores, axis=-1, keepdims=True),
        ),
        jnp.max(fresh_scores, axis=-1, keepdims=True),
    )
    shift = (row_max * score_scale).astype(bf16).astype(f32)

    def weigh(scores, values):
        weights = jnp.exp(scores * score_scale - shift).astype(bf16)
        wide = jnp.concatenate([values, jnp.ones_like(values)], axis=1)
        return dot_nn(weights, wide)

    merged = (
        weigh(slab_scores, new_values)
        + weigh(cache_scores, cache_values)
        + weigh(fresh_scores, fresh_values)
    )
    total = merged[:, HD:]
    high = total.astype(bf16).astype(f32)
    lanes = lax.broadcasted_iota(jnp.int32, (512, HD), 1)
    stats = jnp.where(lanes == 0, shift, jnp.where(lanes == 1, high, total - high))
    out[:, 0:HD] = merged[:, 0:HD].astype(bf16)
    out[:, HD : 2 * HD] = stats.astype(bf16)
    out[:, 2 * HD :] = rebuilt[:, HD:]


def merge(parts, slab, attended):
    heads = []
    rebuilt = []
    for h in range(NX):
        block = parts[h * 128 : (h + 1) * 128, :]
        output = block[:, 0:HD].astype(f32).reshape(16, 8, HD)
        stats = block[:, HD : 2 * HD].astype(f32).reshape(16, 8, HD)
        rebuilt.append(block[:, 2 * HD :])
        shift = stats[:, :, 0:1]
        total = stats[:, :, 1:2] + stats[:, :, 2:3]
        largest = jnp.max(shift, axis=0, keepdims=True)
        factor = jnp.exp(shift - largest)
        merged_total = jnp.sum(factor * total, axis=0)
        merged_output = jnp.sum(factor * output, axis=0)
        heads.append(merged_output / merged_total)
    for h in range(NX):
        for g in range(8):
            start = (h * 8 + g) * HD
            attended[:, start : start + HD] = heads[h][g : g + 1, :].astype(bf16)
    target = lax.broadcasted_iota(jnp.int32, (128, 1), 0)
    origin = (target & 15) * 8 + ((target >> 4) & 3) * 2 + (target >> 6)
    pick = one_hot(origin, 128)
    placed = dot_nn(pick, jnp.concatenate(rebuilt, axis=1)).astype(bf16)
    slab[:, 0:512] = placed[0:64, :]
    slab[:, 512:1024] = placed[64:128, :]


def shift_by(value, axis, step):
    size = lax.axis_size(axis)
    return lax.ppermute(value, axis, [(i, (i + step) % size) for i in range(size)])


def body(
    hidden_slab,
    projection,
    adapter_down,
    adapter_up,
    key_gain,
    cache_keys,
    cache_values,
    fresh_keys,
    fresh_values,
    queries,
    slab_length,
    cache_length,
):
    c = lax.axis_index("c")
    whole = pl.BlockSpec(memory_space=pltpu.VMEM)
    anywhere = pl.BlockSpec(memory_space=pl.ANY)
    rows = hidden_slab[0]

    inputs = [projection, queries[0], fresh_keys[0], fresh_values[0]]
    inputs += [cache_keys[0], cache_values[0]]
    inputs += [cache_length, slab_length.reshape(1, 1)]
    bundle = pl.pallas_call(
        bundle_up,
        in_specs=[anywhere] * 8,
        out_specs=whole,
        out_shape=jax.ShapeDtypeStruct((NX, 288, HD), bf16),
        scratch_shapes=[pltpu.VMEM(a.shape, a.dtype) for a in inputs]
        + [pltpu.SemaphoreType.DMA((8,))],
        compiler_params=pltpu.CompilerParams(vmem_limit_bytes=56 * 1024 * 1024),
    )(*inputs)
    bundle = lax.all_to_all(bundle, "x", 0, 0, tiled=True)

    weight, asked = pl.pallas_call(
        fan_out,
        in_specs=[anywhere],
        out_specs=[whole] * 2,
        out_shape=[
            jax.ShapeDtypeStruct((NY * NZ, 40, 256), bf16),
            jax.ShapeDtypeStruct((NY * NC, 32, HD), bf16),
        ],
        scratch_shapes=[
            pltpu.VMEM((NX, 32, HD), bf16),
            pltpu.SemaphoreType.DMA((1,)),
        ],
        compiler_params=pltpu.CompilerParams(vmem_limit_bytes=8 * 1024 * 1024),
    )(bundle)
    gathered = lax.all_to_all(weight, ("y", "z"), 0, 0, tiled=True)
    left = shift_by(rows, "x", 1)
    right = shift_by(rows, "x", -1)
    far_a = shift_by(left[0:32], "x", 1)
    far_b = shift_by(right[32:64], "x", -1)

    gathered, asked, far_a, far_b = lax.optimization_barrier(
        (gathered.reshape(HALF, 256), asked, far_a, far_b)
    )
    other = shift_by(gathered, "c", 1)
    asked = lax.all_to_all(asked, ("y", "c"), 0, 0, tiled=True)
    rebuilt = pl.pallas_call(
        project,
        in_specs=[anywhere] * 10,
        out_specs=whole,
        out_shape=jax.ShapeDtypeStruct((512, 256), bf16),
        scratch_shapes=[
            pltpu.VMEM((256, 2 * HALF), bf16),
            pltpu.VMEM((NC, HALF, 256), bf16),
            pltpu.VMEM((NX, NY, NC, 80, 256), bf16),
            pltpu.VMEM((64, 2 * HALF), bf16),
            pltpu.VMEM((2, 32, HD), bf16),
            pltpu.VMEM((1, HD), f32),
            pltpu.SemaphoreType.DMA((10,)),
        ],
        compiler_params=pltpu.CompilerParams(vmem_limit_bytes=56 * 1024 * 1024),
        cost_estimate=pl.CostEstimate(
            flops=1400000000, bytes_accessed=8000000, transcendentals=0
        ),
    )(
        rows,
        left,
        far_a,
        far_b,
        right,
        gathered,
        other,
        adapter_down[0].T,
        adapter_up[0],
        key_gain.reshape(1, HD),
    )

    parts = pl.pallas_call(
        attend,
        in_specs=[anywhere] * 3,
        out_specs=whole,
        out_shape=jax.ShapeDtypeStruct((512, 384), bf16),
        scratch_shapes=[
            pltpu.VMEM((NY * NC, 32, HD), bf16),
            pltpu.VMEM((NX, 288, HD), bf16),
            pltpu.VMEM((512, 256), bf16),
            pltpu.SemaphoreType.DMA((3,)),
        ],
        compiler_params=pltpu.CompilerParams(vmem_limit_bytes=16 * 1024 * 1024),
    )(asked, bundle, rebuilt)
    parts = lax.all_to_all(parts.reshape(64, 8, 384), CTX, 0, 0, tiled=True)
    slab, attended = pl.pallas_call(
        merge,
        out_shape=[
            jax.ShapeDtypeStruct((64, 1024), bf16),
            jax.ShapeDtypeStruct((1, 32 * HD), bf16),
        ],
        compiler_params=pltpu.CompilerParams(vmem_limit_bytes=16 * 1024 * 1024),
    )(parts.reshape(512, 384))
    return slab[None], attended[None]


def solution(mesh):
    fine = Mesh(mesh.devices.reshape(NX, NY, NC, NZ), ("x", "y", "c", "z"))
    return jax.shard_map(
        body,
        mesh=fine,
        in_specs=(
            P("z", CTX, None),
            P(CTX + ("z",), None),
            P("z", None, None),
            P("z", None, None, None),
            P(),
            P("z", CTX, None),
            P("z", CTX, None),
            P("z", CTX, None),
            P("z", CTX, None),
            P("z", CTX, None),
            P("z"),
            P("z", CTX),
        ),
        out_specs=(P("z", CTX, None), P("z", CTX, None)),
        check_vma=False,
    )
```

```python
import math

import jax
import jax.numpy as jnp
from jax import lax
from jax.experimental import pallas as pl
from jax.experimental.pallas import tpu as pltpu
from jax.sharding import Mesh, PartitionSpec as P

adapter_scale = 0.5
norm_epsilon = 1e-06
masked_score = -1e30
HD = 128
score_scale = 1.0 / math.sqrt(HD)
NX, NY, NC, NZ = 4, 8, 2, 8
HALF = 2560
CTX = ("x", "y", "c")
bf16 = jnp.bfloat16
f32 = jnp.float32


def dot_nt(a, b):
    return lax.dot_general(a, b, (((1,), (1,)), ((), ())), preferred_element_type=f32)


def dot_nn(a, b):
    return lax.dot_general(a, b, (((1,), (0,)), ((), ())), preferred_element_type=f32)


def one_hot(origin, columns):
    lane = lax.broadcasted_iota(jnp.int32, (origin.shape[0], columns), 1)
    return jnp.where(lane == origin, 1.0, 0.0).astype(bf16)


def fetch(pairs, sems):
    copies = [
        pltpu.make_async_copy(source, target, sems.at[i])
        for i, (source, target) in enumerate(pairs)
    ]
    for copy in copies:
        copy.start()
    return copies


def bundle_up(*refs):
    inputs, bundle, held, sems = refs[0:8], refs[8], refs[9:17], refs[17]
    copies = fetch(list(zip(inputs, held)), sems)
    for copy in copies:
        copy.wait()
    weight, asked, new_key, new_value, keys, values, count, length = [
        ref[...] for ref in held
    ]
    filled = jnp.broadcast_to(count.astype(f32), (1, HD))
    lane = lax.broadcasted_iota(jnp.int32, (1, HD), 1)
    live = jnp.where(lane < 64, length >> 6, length & 63).astype(f32)
    rows = weight.astype(f32)
    small = [ref.astype(f32) for ref in (new_key, new_value, asked)]
    for h in range(NX):
        lanes = slice(h * HD, (h + 1) * HD)
        pieces = [rows[:, lanes], rows[:, 512 + h * HD : 512 + (h + 1) * HD]]
        pieces += [small[0][:, lanes], small[1][:, lanes]]
        pieces += [filled, live]
        for g in range(8):
            start = (h * 8 + g) * HD
            pieces.append(small[2][:, start : start + HD])
        bundle[h, 0:32, :] = jnp.concatenate(pieces, axis=0).astype(bf16)
        bundle[h, 32:160, :] = keys[:, lanes]
        bundle[h, 160:288, :] = values[:, lanes]


def fan_out(bundle, weight, asked, held, sems):
    copy = pltpu.make_async_copy(bundle.at[:, 0:32, :], held, sems.at[0])
    copy.start()
    copy.wait()
    rows = [held[x].astype(f32) for x in range(NX)]
    block = jnp.concatenate([jnp.concatenate([a[0:10], a[10:20]], axis=1) for a in rows])
    block = block.astype(bf16)
    for i in range(NY * NZ):
        weight[i] = block
    block = jnp.concatenate([a[24:32] for a in rows], axis=0).astype(bf16)
    for i in range(NY * NC):
        asked[i] = block


def project(*refs):
    blocks, gathered, other, down_in, up_in, gain_in, out = refs[0:5], *refs[5:11]
    rows, arrived, weight, down, up, gain, sems = refs[11:]
    c = lax.axis_index("c")
    head = lax.axis_index("x")
    up_in = up_in.at[:, :, pl.ds(pl.multiple_of(head * HD, HD), HD)]
    pairs = [(gathered, arrived.at[0]), (other, arrived.at[1])]
    pairs += [(down_in, down), (up_in, up), (gain_in, gain)]
    start = 0
    for block in blocks:
        size = block.shape[0]
        pairs.append((block, rows.at[start : start + size, :]))
        start += size
    copies = fetch(pairs, sems)
    target = lax.broadcasted_iota(jnp.int32, (160, 1), 0)
    x = (target >= 40).astype(jnp.int32)
    x = x + (target >= 80).astype(jnp.int32) + (target >= 120).astype(jnp.int32)
    within = target - 40 * x
    z = (within * 205) >> 11
    pick = one_hot(z * 40 + x * 10 + (within - 10 * z), 160)
    target = lax.broadcasted_iota(jnp.int32, (512, 1), 0)
    at = (head + NX - ((target >> 1) & 3)) & 3
    spread = one_hot((target & 1) * 256 + at * 64 + (target >> 3), 512)
    for side in range(NC):
        core = c if side == 0 else 1 - c
        copies[side].wait()
        for y in range(NY):
            picked = []
            for half in range(2):
                start = y * 320 + half * 160
                picked.append(dot_nn(pick, arrived[side, start : start + 160, :]))
            for x in range(NX):
                own = [a[x * 40 : (x + 1) * 40] for a in picked]
                weight[x, y, core] = jnp.concatenate(own, axis=0).astype(bf16)
    for copy in copies[2:]:
        copy.wait()
    low = dot_nt(rows[...], down[...]).astype(bf16)
    base = dot_nn(rows[...], weight[...].reshape(2 * HALF, 256))
    raw_keys = base[:, 0:HD] + adapter_scale * dot_nn(low[:, 0:32], up[0])
    new_values = base[:, HD:] + adapter_scale * dot_nn(low[:, 32:64], up[1])
    mean = jnp.mean(raw_keys * raw_keys, axis=-1, keepdims=True)
    new_keys = raw_keys * lax.rsqrt(mean + norm_epsilon) * gain[...]
    rebuilt = jnp.concatenate([new_keys, new_values], axis=0).astype(bf16)
    out[:, 0:HD] = rebuilt
    out[:, HD:] = dot_nn(spread, rebuilt).astype(bf16)


def attend(*refs):
    asked, bundle, rebuilt, out = refs
    head = lax.axis_index("x")
    y = lax.axis_index("y")
    c = lax.axis_index("c")
    queries = asked[...].astype(f32).reshape(NY * NC, NX, 8, HD)
    queries = jnp.stack([queries[:, i] for i in range(NX)], axis=0)
    queries = queries.reshape(512, HD).astype(bf16)

    cache_keys = bundle[:, 32:160, :].reshape(512, HD)
    cache_values = bundle[:, 160:288, :].reshape(512, HD)
    lane = lax.broadcasted_iota(jnp.int32, (1, HD), 1).astype(f32)
    news = [bundle[i, 16:32, :].astype(f32) for i in range(NX)]
    filled = jnp.concatenate(
        [jnp.where(lane < new[6:7, :], 1.0, 0.0) for new in news], axis=1
    )
    cache_scores = jnp.where(filled > 0.5, dot_nt(queries, cache_keys), masked_score)
    fresh_keys = jnp.concatenate([new[4:5, :] for new in news] * 2, axis=0)
    fresh_values = jnp.concatenate([new[5:6, :] for new in news] * 2, axis=0)
    fresh_keys = fresh_keys.astype(bf16)
    fresh_values = fresh_values.astype(bf16)
    token = lax.broadcasted_iota(jnp.int32, (512, 8), 0) >> 3
    fresh_at = lax.broadcasted_iota(jnp.int32, (1, 8), 1)
    fresh_ok = (fresh_at < NX) & (fresh_at * 16 + y * 2 + c <= token)
    fresh_scores = jnp.where(fresh_ok, dot_nt(queries, fresh_keys), masked_score)

    new_keys = rebuilt[0:256, 0:HD]
    new_values = rebuilt[256:512, 0:HD]
    column = lax.broadcasted_iota(jnp.int32, (1, 256), 1)
    shard = (head + NX - (column >> 6)) & 3
    initial = shard * 1024 + (y * 2 + c) * 64 + (column & 63)
    slab_length = news[0][7:8, 0:1] * 64.0 + news[0][7:8, 64:65]
    live = initial.astype(f32) < slab_length
    slab_scores = jnp.where(
        live, dot_nt(queries, new_keys), masked_score
    )

    row_max = jnp.maximum(
        jnp.maximum(
            jnp.max(slab_scores, axis=-1, keepdims=True),
            jnp.max(cache_scores, axis=-1, keepdims=True),
        ),
        jnp.max(fresh_scores, axis=-1, keepdims=True),
    )
    shift = (row_max * score_scale).astype(bf16).astype(f32)

    def weigh(scores, values):
        weights = jnp.exp(scores * score_scale - shift).astype(bf16)
        wide = jnp.concatenate([values, jnp.ones_like(values)], axis=1)
        return dot_nn(weights, wide)

    merged = (
        weigh(slab_scores, new_values)
        + weigh(cache_scores, cache_values)
        + weigh(fresh_scores, fresh_values)
    )
    total = merged[:, HD:]
    high = total.astype(bf16).astype(f32)
    lanes = lax.broadcasted_iota(jnp.int32, (512, HD), 1)
    stats = jnp.where(lanes == 0, shift, jnp.where(lanes == 1, high, total - high))
    out[:, 0:HD] = merged[:, 0:HD].astype(bf16)
    out[:, HD : 2 * HD] = stats.astype(bf16)
    out[:, 2 * HD :] = rebuilt[:, HD:]


def merge(parts, slab, attended):
    heads = []
    rebuilt = []
    for h in range(NX):
        block = parts[h * 128 : (h + 1) * 128, :]
        output = block[:, 0:HD].astype(f32).reshape(16, 8, HD)
        stats = block[:, HD : 2 * HD].astype(f32).reshape(16, 8, HD)
        rebuilt.append(block[:, 2 * HD :])
        shift = stats[:, :, 0:1]
        total = stats[:, :, 1:2] + stats[:, :, 2:3]
        largest = jnp.max(shift, axis=0, keepdims=True)
        factor = jnp.exp(shift - largest)
        merged_total = jnp.sum(factor * total, axis=0)
        merged_output = jnp.sum(factor * output, axis=0)
        heads.append(merged_output / merged_total)
    for h in range(NX):
        for g in range(8):
            start = (h * 8 + g) * HD
            attended[:, start : start + HD] = heads[h][g : g + 1, :].astype(bf16)
    target = lax.broadcasted_iota(jnp.int32, (128, 1), 0)
    origin = (target & 15) * 8 + ((target >> 4) & 3) * 2 + (target >> 6)
    pick = one_hot(origin, 128)
    placed = dot_nn(pick, jnp.concatenate(rebuilt, axis=1)).astype(bf16)
    slab[:, 0:512] = placed[0:64, :]
    slab[:, 512:1024] = placed[64:128, :]


def shift_by(value, axis, step):
    size = lax.axis_size(axis)
    return lax.ppermute(value, axis, [(i, (i + step) % size) for i in range(size)])


def body(
    hidden_slab,
    projection,
    adapter_down,
    adapter_up,
    key_gain,
    cache_keys,
    cache_values,
    fresh_keys,
    fresh_values,
    queries,
    slab_length,
    cache_length,
):
    c = lax.axis_index("c")
    whole = pl.BlockSpec(memory_space=pltpu.VMEM)
    anywhere = pl.BlockSpec(memory_space=pl.ANY)
    rows = hidden_slab[0]

    inputs = [projection, queries[0], fresh_keys[0], fresh_values[0]]
    inputs += [cache_keys[0], cache_values[0]]
    inputs += [cache_length, slab_length.reshape(1, 1)]
    bundle = pl.pallas_call(
        bundle_up,
        in_specs=[anywhere] * 8,
        out_specs=whole,
        out_shape=jax.ShapeDtypeStruct((NX, 288, HD), bf16),
        scratch_shapes=[pltpu.VMEM(a.shape, a.dtype) for a in inputs]
        + [pltpu.SemaphoreType.DMA((8,))],
        compiler_params=pltpu.CompilerParams(vmem_limit_bytes=56 * 1024 * 1024),
    )(*inputs)
    bundle = lax.all_to_all(bundle, "x", 0, 0, tiled=True)

    weight, asked = pl.pallas_call(
        fan_out,
        in_specs=[anywhere],
        out_specs=[whole] * 2,
        out_shape=[
            jax.ShapeDtypeStruct((NY * NZ, 40, 256), bf16),
            jax.ShapeDtypeStruct((NY * NC, 32, HD), bf16),
        ],
        scratch_shapes=[
            pltpu.VMEM((NX, 32, HD), bf16),
            pltpu.SemaphoreType.DMA((1,)),
        ],
        compiler_params=pltpu.CompilerParams(vmem_limit_bytes=8 * 1024 * 1024),
    )(bundle)
    gathered = lax.all_to_all(weight, ("y", "z"), 0, 0, tiled=True)
    left = shift_by(rows, "x", 1)
    right = shift_by(rows, "x", -1)
    far_a = shift_by(left[0:32], "x", 1)
    far_b = shift_by(right[32:64], "x", -1)

    gathered, asked, far_a, far_b = lax.optimization_barrier(
        (gathered.reshape(HALF, 256), asked, far_a, far_b)
    )
    other = shift_by(gathered, "c", 1)
    asked = lax.all_to_all(asked, ("y", "c"), 0, 0, tiled=True)
    rebuilt = pl.pallas_call(
        project,
        in_specs=[anywhere] * 10,
        out_specs=whole,
        out_shape=jax.ShapeDtypeStruct((512, 256), bf16),
        scratch_shapes=[
            pltpu.VMEM((256, 2 * HALF), bf16),
            pltpu.VMEM((NC, HALF, 256), bf16),
            pltpu.VMEM((NX, NY, NC, 80, 256), bf16),
            pltpu.VMEM((64, 2 * HALF), bf16),
            pltpu.VMEM((2, 32, HD), bf16),
            pltpu.VMEM((1, HD), f32),
            pltpu.SemaphoreType.DMA((10,)),
        ],
        compiler_params=pltpu.CompilerParams(vmem_limit_bytes=56 * 1024 * 1024),
        cost_estimate=pl.CostEstimate(
            flops=1400000000, bytes_accessed=8000000, transcendentals=0
        ),
    )(
        rows,
        left,
        far_a,
        far_b,
        right,
        gathered,
        other,
        adapter_down[0].T,
        adapter_up[0],
        key_gain.reshape(1, HD),
    )

    parts = pl.pallas_call(
        attend,
        in_specs=[whole] * 3,
        out_specs=whole,
        out_shape=jax.ShapeDtypeStruct((512, 384), bf16),
        compiler_params=pltpu.CompilerParams(vmem_limit_bytes=16 * 1024 * 1024),
    )(asked, bundle, rebuilt)
    parts = lax.all_to_all(parts.reshape(64, 8, 384), CTX, 0, 0, tiled=True)
    slab, attended = pl.pallas_call(
        merge,
        out_shape=[
            jax.ShapeDtypeStruct((64, 1024), bf16),
            jax.ShapeDtypeStruct((1, 32 * HD), bf16),
        ],
        compiler_params=pltpu.CompilerParams(vmem_limit_bytes=16 * 1024 * 1024),
    )(parts.reshape(512, 384))
    return slab[None], attended[None]


def solution(mesh):
    fine = Mesh(mesh.devices.reshape(NX, NY, NC, NZ), ("x", "y", "c", "z"))
    return jax.shard_map(
        body,
        mesh=fine,
        in_specs=(
            P("z", CTX, None),
            P(CTX + ("z",), None),
            P("z", None, None),
            P("z", None, None, None),
            P(),
            P("z", CTX, None),
            P("z", CTX, None),
            P("z", CTX, None),
            P("z", CTX, None),
            P("z", CTX, None),
            P("z"),
            P("z", CTX),
        ),
        out_specs=(P("z", CTX, None), P("z", CTX, None)),
        check_vma=False,
    )
```

```python
import math

import jax
import jax.numpy as jnp
from jax import lax
from jax.experimental import pallas as pl
from jax.experimental.pallas import tpu as pltpu
from jax.sharding import Mesh, PartitionSpec as P

adapter_scale = 0.5
norm_epsilon = 1e-06
masked_score = -1e30
HD = 128
score_scale = 1.0 / math.sqrt(HD)
NX, NY, NC, NZ = 4, 8, 2, 8
HALF = 2560
CTX = ("x", "y", "c")
bf16 = jnp.bfloat16
f32 = jnp.float32


def dot_nt(a, b):
    return lax.dot_general(a, b, (((1,), (1,)), ((), ())), preferred_element_type=f32)


def dot_nn(a, b):
    return lax.dot_general(a, b, (((1,), (0,)), ((), ())), preferred_element_type=f32)


def one_hot(origin, columns):
    lane = lax.broadcasted_iota(jnp.int32, (origin.shape[0], columns), 1)
    return jnp.where(lane == origin, 1.0, 0.0).astype(bf16)


def fetch(pairs, sems):
    copies = [
        pltpu.make_async_copy(source, target, sems.at[i])
        for i, (source, target) in enumerate(pairs)
    ]
    for copy in copies:
        copy.start()
    return copies


def bundle_up(*refs):
    inputs, bundle, held, sems = refs[0:8], refs[8], refs[9:17], refs[17]
    copies = fetch(list(zip(inputs, held)), sems)
    for copy in copies:
        copy.wait()
    weight, asked, new_key, new_value, keys, values, count, length = [
        ref[...] for ref in held
    ]
    filled = jnp.broadcast_to(count.astype(f32), (1, HD))
    lane = lax.broadcasted_iota(jnp.int32, (1, HD), 1)
    live = jnp.where(lane < 64, length >> 6, length & 63).astype(f32)
    rows = weight.astype(f32)
    small = [ref.astype(f32) for ref in (new_key, new_value, asked)]
    for h in range(NX):
        lanes = slice(h * HD, (h + 1) * HD)
        pieces = [rows[:, lanes], rows[:, 512 + h * HD : 512 + (h + 1) * HD]]
        pieces += [small[0][:, lanes], small[1][:, lanes]]
        pieces += [filled, live]
        for g in range(8):
            start = (h * 8 + g) * HD
            pieces.append(small[2][:, start : start + HD])
        bundle[h, 0:32, :] = jnp.concatenate(pieces, axis=0).astype(bf16)
        bundle[h, 32:160, :] = keys[:, lanes]
        bundle[h, 160:288, :] = values[:, lanes]


def fan_out(bundle, weight, asked, held, sems):
    copy = pltpu.make_async_copy(bundle.at[:, 0:32, :], held, sems.at[0])
    copy.start()
    copy.wait()
    rows = [held[x].astype(f32) for x in range(NX)]
    block = jnp.concatenate([jnp.concatenate([a[0:10], a[10:20]], axis=1) for a in rows])
    block = block.astype(bf16)
    for i in range(NY * NZ):
        weight[i] = block
    block = jnp.concatenate([a[24:32] for a in rows], axis=0).astype(bf16)
    for i in range(NY * NC):
        asked[i] = block


def project(*refs):
    blocks, gathered, other, down_in, up_in, gain_in, out = refs[0:5], *refs[5:11]
    rows, arrived, weight, down, up, gain, sems = refs[11:]
    c = lax.axis_index("c")
    head = lax.axis_index("x")
    up_in = up_in.at[:, :, pl.ds(pl.multiple_of(head * HD, HD), HD)]
    pairs = [(gathered, arrived.at[0]), (other, arrived.at[1])]
    pairs += [(down_in, down), (up_in, up), (gain_in, gain)]
    start = 0
    for block in blocks:
        size = block.shape[0]
        pairs.append((block, rows.at[start : start + size, :]))
        start += size
    copies = fetch(pairs, sems)
    target = lax.broadcasted_iota(jnp.int32, (160, 1), 0)
    x = (target >= 40).astype(jnp.int32)
    x = x + (target >= 80).astype(jnp.int32) + (target >= 120).astype(jnp.int32)
    within = target - 40 * x
    z = (within * 205) >> 11
    pick = one_hot(z * 40 + x * 10 + (within - 10 * z), 160)
    target = lax.broadcasted_iota(jnp.int32, (512, 1), 0)
    at = (head + NX - ((target >> 1) & 3)) & 3
    spread = one_hot((target & 1) * 256 + at * 64 + (target >> 3), 512)
    for side in range(NC):
        core = c if side == 0 else 1 - c
        copies[side].wait()
        for y in range(NY):
            picked = []
            for half in range(2):
                start = y * 320 + half * 160
                picked.append(dot_nn(pick, arrived[side, start : start + 160, :]))
            for x in range(NX):
                own = [a[x * 40 : (x + 1) * 40] for a in picked]
                weight[x, y, core] = jnp.concatenate(own, axis=0).astype(bf16)
    for copy in copies[2:]:
        copy.wait()
    low = dot_nt(rows[...], down[...]).astype(bf16)
    base = dot_nn(rows[...], weight[...].reshape(2 * HALF, 256))
    raw_keys = base[:, 0:HD] + adapter_scale * dot_nn(low[:, 0:32], up[0])
    new_values = base[:, HD:] + adapter_scale * dot_nn(low[:, 32:64], up[1])
    mean = jnp.mean(raw_keys * raw_keys, axis=-1, keepdims=True)
    new_keys = raw_keys * lax.rsqrt(mean + norm_epsilon) * gain[...]
    rebuilt = jnp.concatenate([new_keys, new_values], axis=0).astype(bf16)
    out[:, 0:HD] = rebuilt
    out[:, HD:] = dot_nn(spread, rebuilt).astype(bf16)


def attend(*refs):
    asked, bundle, rebuilt, out = refs
    head = lax.axis_index("x")
    y = lax.axis_index("y")
    c = lax.axis_index("c")
    queries = asked[...].astype(f32).reshape(NY * NC, NX, 8, HD)
    queries = jnp.stack([queries[:, i] for i in range(NX)], axis=0)
    queries = queries.reshape(512, HD).astype(bf16)

    cache_keys = bundle[:, 32:160, :].reshape(512, HD)
    cache_values = bundle[:, 160:288, :].reshape(512, HD)
    lane = lax.broadcasted_iota(jnp.int32, (1, HD), 1).astype(f32)
    news = [bundle[i, 16:32, :].astype(f32) for i in range(NX)]
    filled = jnp.concatenate(
        [jnp.where(lane < new[6:7, :], 1.0, 0.0) for new in news], axis=1
    )
    cache_scores = jnp.where(filled > 0.5, dot_nt(queries, cache_keys), masked_score)
    fresh_keys = jnp.concatenate([new[4:5, :] for new in news] * 2, axis=0)
    fresh_values = jnp.concatenate([new[5:6, :] for new in news] * 2, axis=0)
    fresh_keys = fresh_keys.astype(bf16)
    fresh_values = fresh_values.astype(bf16)
    token = lax.broadcasted_iota(jnp.int32, (512, 8), 0) >> 3
    fresh_at = lax.broadcasted_iota(jnp.int32, (1, 8), 1)
    fresh_ok = (fresh_at < NX) & (fresh_at * 16 + y * 2 + c <= token)
    fresh_scores = jnp.where(fresh_ok, dot_nt(queries, fresh_keys), masked_score)

    new_keys = rebuilt[0:256, 0:HD]
    new_values = rebuilt[256:512, 0:HD]
    column = lax.broadcasted_iota(jnp.int32, (1, 256), 1)
    shard = (head + NX - (column >> 6)) & 3
    initial = shard * 1024 + (y * 2 + c) * 64 + (column & 63)
    slab_length = news[0][7:8, 0:1] * 64.0 + news[0][7:8, 64:65]
    live = initial.astype(f32) < slab_length
    slab_scores = jnp.where(
        live, dot_nt(queries, new_keys), masked_score
    )

    row_max = jnp.maximum(
        jnp.maximum(
            jnp.max(slab_scores, axis=-1, keepdims=True),
            jnp.max(cache_scores, axis=-1, keepdims=True),
        ),
        jnp.max(fresh_scores, axis=-1, keepdims=True),
    )
    shift = (row_max * score_scale).astype(bf16).astype(f32)

    def weigh(scores, values):
        weights = jnp.exp(scores * score_scale - shift).astype(bf16)
        wide = jnp.concatenate([values, jnp.ones_like(values)], axis=1)
        return dot_nn(weights, wide)

    merged = (
        weigh(slab_scores, new_values)
        + weigh(cache_scores, cache_values)
        + weigh(fresh_scores, fresh_values)
    )
    total = merged[:, HD:]
    high = total.astype(bf16).astype(f32)
    lanes = lax.broadcasted_iota(jnp.int32, (512, HD), 1)
    stats = jnp.where(lanes == 0, shift, jnp.where(lanes == 1, high, total - high))
    out[:, 0:HD] = merged[:, 0:HD].astype(bf16)
    out[:, HD : 2 * HD] = stats.astype(bf16)
    out[:, 2 * HD :] = rebuilt[:, HD:]


def merge(parts, slab, attended):
    heads = []
    rebuilt = []
    for h in range(NX):
        block = parts[h * 128 : (h + 1) * 128, :]
        output = block[:, 0:HD].astype(f32).reshape(16, 8, HD)
        stats = block[:, HD : 2 * HD].astype(f32).reshape(16, 8, HD)
        rebuilt.append(block[:, 2 * HD :])
        shift = stats[:, :, 0:1]
        total = stats[:, :, 1:2] + stats[:, :, 2:3]
        largest = jnp.max(shift, axis=0, keepdims=True)
        factor = jnp.exp(shift - largest)
        merged_total = jnp.sum(factor * total, axis=0)
        merged_output = jnp.sum(factor * output, axis=0)
        heads.append(merged_output / merged_total)
    for h in range(NX):
        for g in range(8):
            start = (h * 8 + g) * HD
            attended[:, start : start + HD] = heads[h][g : g + 1, :].astype(bf16)
    target = lax.broadcasted_iota(jnp.int32, (128, 1), 0)
    origin = (target & 15) * 8 + ((target >> 4) & 3) * 2 + (target >> 6)
    pick = one_hot(origin, 128)
    placed = dot_nn(pick, jnp.concatenate(rebuilt, axis=1)).astype(bf16)
    slab[:, 0:512] = placed[0:64, :]
    slab[:, 512:1024] = placed[64:128, :]


def shift_by(value, axis, step):
    size = lax.axis_size(axis)
    return lax.ppermute(value, axis, [(i, (i + step) % size) for i in range(size)])


def body(
    hidden_slab,
    projection,
    adapter_down,
    adapter_up,
    key_gain,
    cache_keys,
    cache_values,
    fresh_keys,
    fresh_values,
    queries,
    slab_length,
    cache_length,
):
    c = lax.axis_index("c")
    whole = pl.BlockSpec(memory_space=pltpu.VMEM)
    anywhere = pl.BlockSpec(memory_space=pl.ANY)
    rows = hidden_slab[0]

    inputs = [projection, queries[0], fresh_keys[0], fresh_values[0]]
    inputs += [cache_keys[0], cache_values[0]]
    inputs += [cache_length, slab_length.reshape(1, 1)]
    bundle = pl.pallas_call(
        bundle_up,
        in_specs=[anywhere] * 8,
        out_specs=whole,
        out_shape=jax.ShapeDtypeStruct((NX, 288, HD), bf16),
        scratch_shapes=[pltpu.VMEM(a.shape, a.dtype) for a in inputs]
        + [pltpu.SemaphoreType.DMA((8,))],
        compiler_params=pltpu.CompilerParams(vmem_limit_bytes=56 * 1024 * 1024),
    )(*inputs)
    bundle = lax.all_to_all(bundle, "x", 0, 0, tiled=True)

    weight, asked = pl.pallas_call(
        fan_out,
        in_specs=[anywhere],
        out_specs=[whole] * 2,
        out_shape=[
            jax.ShapeDtypeStruct((NY * NZ, 40, 256), bf16),
            jax.ShapeDtypeStruct((NY * NC, 32, HD), bf16),
        ],
        scratch_shapes=[
            pltpu.VMEM((NX, 32, HD), bf16),
            pltpu.SemaphoreType.DMA((1,)),
        ],
        compiler_params=pltpu.CompilerParams(vmem_limit_bytes=8 * 1024 * 1024),
    )(bundle)
    gathered = lax.all_to_all(weight, ("y", "z"), 0, 0, tiled=True)
    left = shift_by(rows, "x", 1)
    right = shift_by(rows, "x", -1)
    far_a = shift_by(left[0:16], "x", 1)
    far_b = shift_by(right[16:64], "x", -1)

    gathered, asked, far_a, far_b = lax.optimization_barrier(
        (gathered.reshape(HALF, 256), asked, far_a, far_b)
    )
    other = shift_by(gathered, "c", 1)
    asked = lax.all_to_all(asked, ("y", "c"), 0, 0, tiled=True)
    rebuilt = pl.pallas_call(
        project,
        in_specs=[anywhere] * 10,
        out_specs=whole,
        out_shape=jax.ShapeDtypeStruct((512, 256), bf16),
        scratch_shapes=[
            pltpu.VMEM((256, 2 * HALF), bf16),
            pltpu.VMEM((NC, HALF, 256), bf16),
            pltpu.VMEM((NX, NY, NC, 80, 256), bf16),
            pltpu.VMEM((64, 2 * HALF), bf16),
            pltpu.VMEM((2, 32, HD), bf16),
            pltpu.VMEM((1, HD), f32),
            pltpu.SemaphoreType.DMA((10,)),
        ],
        compiler_params=pltpu.CompilerParams(vmem_limit_bytes=56 * 1024 * 1024),
        cost_estimate=pl.CostEstimate(
            flops=1400000000, bytes_accessed=8000000, transcendentals=0
        ),
    )(
        rows,
        left,
        far_a,
        far_b,
        right,
        gathered,
        other,
        adapter_down[0].T,
        adapter_up[0],
        key_gain.reshape(1, HD),
    )

    parts = pl.pallas_call(
        attend,
        in_specs=[whole] * 3,
        out_specs=whole,
        out_shape=jax.ShapeDtypeStruct((512, 384), bf16),
        compiler_params=pltpu.CompilerParams(vmem_limit_bytes=16 * 1024 * 1024),
    )(asked, bundle, rebuilt)
    parts = lax.all_to_all(parts.reshape(64, 8, 384), CTX, 0, 0, tiled=True)
    slab, attended = pl.pallas_call(
        merge,
        out_shape=[
            jax.ShapeDtypeStruct((64, 1024), bf16),
            jax.ShapeDtypeStruct((1, 32 * HD), bf16),
        ],
        compiler_params=pltpu.CompilerParams(vmem_limit_bytes=16 * 1024 * 1024),
    )(parts.reshape(512, 384))
    return slab[None], attended[None]


def solution(mesh):
    fine = Mesh(mesh.devices.reshape(NX, NY, NC, NZ), ("x", "y", "c", "z"))
    return jax.shard_map(
        body,
        mesh=fine,
        in_specs=(
            P("z", CTX, None),
            P(CTX + ("z",), None),
            P("z", None, None),
            P("z", None, None, None),
            P(),
            P("z", CTX, None),
            P("z", CTX, None),
            P("z", CTX, None),
            P("z", CTX, None),
            P("z", CTX, None),
            P("z"),
            P("z", CTX),
        ),
        out_specs=(P("z", CTX, None), P("z", CTX, None)),
        check_vma=False,
    )
```

```python
import math

import jax
import jax.numpy as jnp
from jax import lax
from jax.experimental import pallas as pl
from jax.experimental.pallas import tpu as pltpu
from jax.sharding import Mesh, PartitionSpec as P

adapter_scale = 0.5
norm_epsilon = 1e-06
masked_score = -1e30
HD = 128
score_scale = 1.0 / math.sqrt(HD)
NX, NY, NC, NZ = 4, 8, 2, 8
HALF = 2560
CTX = ("x", "y", "c")
bf16 = jnp.bfloat16
f32 = jnp.float32


def dot_nt(a, b):
    return lax.dot_general(a, b, (((1,), (1,)), ((), ())), preferred_element_type=f32)


def dot_nn(a, b):
    return lax.dot_general(a, b, (((1,), (0,)), ((), ())), preferred_element_type=f32)


def one_hot(origin, columns):
    lane = lax.broadcasted_iota(jnp.int32, (origin.shape[0], columns), 1)
    return jnp.where(lane == origin, 1.0, 0.0).astype(bf16)


def fetch(pairs, sems):
    copies = [
        pltpu.make_async_copy(source, target, sems.at[i])
        for i, (source, target) in enumerate(pairs)
    ]
    for copy in copies:
        copy.start()
    return copies


def bundle_up(*refs):
    inputs, bundle, held, sems = refs[0:8], refs[8], refs[9:17], refs[17]
    copies = fetch(list(zip(inputs, held)), sems)
    for copy in copies:
        copy.wait()
    weight, asked, new_key, new_value, keys, values, count, length = [
        ref[...] for ref in held
    ]
    filled = jnp.broadcast_to(count.astype(f32), (1, HD))
    lane = lax.broadcasted_iota(jnp.int32, (1, HD), 1)
    live = jnp.where(lane < 64, length >> 6, length & 63).astype(f32)
    rows = weight.astype(f32)
    small = [ref.astype(f32) for ref in (new_key, new_value, asked)]
    for h in range(NX):
        lanes = slice(h * HD, (h + 1) * HD)
        pieces = [rows[:, lanes], rows[:, 512 + h * HD : 512 + (h + 1) * HD]]
        pieces += [small[0][:, lanes], small[1][:, lanes]]
        pieces += [filled, live]
        for g in range(8):
            start = (h * 8 + g) * HD
            pieces.append(small[2][:, start : start + HD])
        bundle[h, 0:32, :] = jnp.concatenate(pieces, axis=0).astype(bf16)
        bundle[h, 32:160, :] = keys[:, lanes]
        bundle[h, 160:288, :] = values[:, lanes]


def fan_out(bundle, weight, asked, held, sems):
    copy = pltpu.make_async_copy(bundle.at[:, 0:32, :], held, sems.at[0])
    copy.start()
    copy.wait()
    rows = [held[x].astype(f32) for x in range(NX)]
    block = jnp.concatenate([jnp.concatenate([a[0:10], a[10:20]], axis=1) for a in rows])
    block = block.astype(bf16)
    for i in range(NY * NZ):
        weight[i] = block
    block = jnp.concatenate([a[24:32] for a in rows], axis=0).astype(bf16)
    for i in range(NY * NC):
        asked[i] = block


def project(*refs):
    blocks, gathered, other, down_in, up_in, gain_in, out = refs[0:5], *refs[5:11]
    rows, arrived, weight, down, up, gain, sems = refs[11:]
    c = lax.axis_index("c")
    head = lax.axis_index("x")
    up_in = up_in.at[:, :, pl.ds(pl.multiple_of(head * HD, HD), HD)]
    pairs = [(gathered, arrived.at[0]), (other, arrived.at[1])]
    pairs += [(down_in, down), (up_in, up), (gain_in, gain)]
    start = 0
    for block in blocks:
        size = block.shape[0]
        pairs.append((block, rows.at[start : start + size, :]))
        start += size
    copies = fetch(pairs, sems)
    target = lax.broadcasted_iota(jnp.int32, (160, 1), 0)
    x = (target >= 40).astype(jnp.int32)
    x = x + (target >= 80).astype(jnp.int32) + (target >= 120).astype(jnp.int32)
    within = target - 40 * x
    z = (within * 205) >> 11
    pick = one_hot(z * 40 + x * 10 + (within - 10 * z), 160)
    target = lax.broadcasted_iota(jnp.int32, (512, 1), 0)
    at = (head + NX - ((target >> 1) & 3)) & 3
    spread = one_hot((target & 1) * 256 + at * 64 + (target >> 3), 512)
    for side in range(NC):
        core = c if side == 0 else 1 - c
        copies[side].wait()
        for y in range(NY):
            picked = []
            for half in range(2):
                start = y * 320 + half * 160
                picked.append(dot_nn(pick, arrived[side, start : start + 160, :]))
            for x in range(NX):
                own = [a[x * 40 : (x + 1) * 40] for a in picked]
                weight[x, y, core] = jnp.concatenate(own, axis=0).astype(bf16)
    for copy in copies[2:]:
        copy.wait()
    low = dot_nt(rows[...], down[...]).astype(bf16)
    base = dot_nn(rows[...], weight[...].reshape(2 * HALF, 256))
    raw_keys = base[:, 0:HD] + adapter_scale * dot_nn(low[:, 0:32], up[0])
    new_values = base[:, HD:] + adapter_scale * dot_nn(low[:, 32:64], up[1])
    mean = jnp.mean(raw_keys * raw_keys, axis=-1, keepdims=True)
    new_keys = raw_keys * lax.rsqrt(mean + norm_epsilon) * gain[...]
    rebuilt = jnp.concatenate([new_keys, new_values], axis=0).astype(bf16)
    out[:, 0:HD] = rebuilt
    out[:, HD:] = dot_nn(spread, rebuilt).astype(bf16)


def attend(*refs):
    asked, bundle, rebuilt, out = refs
    head = lax.axis_index("x")
    y = lax.axis_index("y")
    c = lax.axis_index("c")
    queries = asked[...].astype(f32).reshape(NY * NC, NX, 8, HD)
    queries = jnp.stack([queries[:, i] for i in range(NX)], axis=0)
    queries = queries.reshape(512, HD).astype(bf16)

    cache_keys = bundle[:, 32:160, :].reshape(512, HD)
    cache_values = bundle[:, 160:288, :].reshape(512, HD)
    lane = lax.broadcasted_iota(jnp.int32, (1, HD), 1).astype(f32)
    news = [bundle[i, 16:32, :].astype(f32) for i in range(NX)]
    filled = jnp.concatenate(
        [jnp.where(lane < new[6:7, :], 1.0, 0.0) for new in news], axis=1
    )
    cache_scores = jnp.where(filled > 0.5, dot_nt(queries, cache_keys), masked_score)
    fresh_keys = jnp.concatenate([new[4:5, :] for new in news] * 2, axis=0)
    fresh_values = jnp.concatenate([new[5:6, :] for new in news] * 2, axis=0)
    fresh_keys = fresh_keys.astype(bf16)
    fresh_values = fresh_values.astype(bf16)
    token = lax.broadcasted_iota(jnp.int32, (512, 8), 0) >> 3
    fresh_at = lax.broadcasted_iota(jnp.int32, (1, 8), 1)
    fresh_ok = (fresh_at < NX) & (fresh_at * 16 + y * 2 + c <= token)
    fresh_scores = jnp.where(fresh_ok, dot_nt(queries, fresh_keys), masked_score)

    new_keys = rebuilt[0:256, 0:HD]
    new_values = rebuilt[256:512, 0:HD]
    column = lax.broadcasted_iota(jnp.int32, (1, 256), 1)
    shard = (head + NX - (column >> 6)) & 3
    initial = shard * 1024 + (y * 2 + c) * 64 + (column & 63)
    slab_length = news[0][7:8, 0:1] * 64.0 + news[0][7:8, 64:65]
    live = initial.astype(f32) < slab_length
    slab_scores = jnp.where(
        live, dot_nt(queries, new_keys), masked_score
    )

    row_max = jnp.maximum(
        jnp.maximum(
            jnp.max(slab_scores, axis=-1, keepdims=True),
            jnp.max(cache_scores, axis=-1, keepdims=True),
        ),
        jnp.max(fresh_scores, axis=-1, keepdims=True),
    )
    shift = (row_max * score_scale).astype(bf16).astype(f32)

    def weigh(scores, values):
        weights = jnp.exp(scores * score_scale - shift).astype(bf16)
        wide = jnp.concatenate([values, jnp.ones_like(values)], axis=1)
        return dot_nn(weights, wide)

    merged = (
        weigh(slab_scores, new_values)
        + weigh(cache_scores, cache_values)
        + weigh(fresh_scores, fresh_values)
    )
    total = merged[:, HD:]
    high = total.astype(bf16).astype(f32)
    lanes = lax.broadcasted_iota(jnp.int32, (512, HD), 1)
    stats = jnp.where(lanes == 0, shift, jnp.where(lanes == 1, high, total - high))
    out[:, 0:HD] = merged[:, 0:HD].astype(bf16)
    out[:, HD : 2 * HD] = stats.astype(bf16)
    out[:, 2 * HD :] = rebuilt[:, HD:]


def merge(parts, slab, attended):
    heads = []
    rebuilt = []
    for h in range(NX):
        block = parts[h * 128 : (h + 1) * 128, :]
        output = block[:, 0:HD].astype(f32).reshape(16, 8, HD)
        stats = block[:, HD : 2 * HD].astype(f32).reshape(16, 8, HD)
        rebuilt.append(block[:, 2 * HD :])
        shift = stats[:, :, 0:1]
        total = stats[:, :, 1:2] + stats[:, :, 2:3]
        largest = jnp.max(shift, axis=0, keepdims=True)
        factor = jnp.exp(shift - largest)
        merged_total = jnp.sum(factor * total, axis=0)
        merged_output = jnp.sum(factor * output, axis=0)
        heads.append(merged_output / merged_total)
    for h in range(NX):
        for g in range(8):
            start = (h * 8 + g) * HD
            attended[:, start : start + HD] = heads[h][g : g + 1, :].astype(bf16)
    target = lax.broadcasted_iota(jnp.int32, (128, 1), 0)
    origin = (target & 15) * 8 + ((target >> 4) & 3) * 2 + (target >> 6)
    pick = one_hot(origin, 128)
    placed = dot_nn(pick, jnp.concatenate(rebuilt, axis=1)).astype(bf16)
    slab[:, 0:512] = placed[0:64, :]
    slab[:, 512:1024] = placed[64:128, :]


def shift_by(value, axis, step):
    size = lax.axis_size(axis)
    return lax.ppermute(value, axis, [(i, (i + step) % size) for i in range(size)])


def body(
    hidden_slab,
    projection,
    adapter_down,
    adapter_up,
    key_gain,
    cache_keys,
    cache_values,
    fresh_keys,
    fresh_values,
    queries,
    slab_length,
    cache_length,
):
    c = lax.axis_index("c")
    whole = pl.BlockSpec(memory_space=pltpu.VMEM)
    anywhere = pl.BlockSpec(memory_space=pl.ANY)
    rows = hidden_slab[0]

    inputs = [projection, queries[0], fresh_keys[0], fresh_values[0]]
    inputs += [cache_keys[0], cache_values[0]]
    inputs += [cache_length, slab_length.reshape(1, 1)]
    bundle = pl.pallas_call(
        bundle_up,
        in_specs=[anywhere] * 8,
        out_specs=whole,
        out_shape=jax.ShapeDtypeStruct((NX, 288, HD), bf16),
        scratch_shapes=[pltpu.VMEM(a.shape, a.dtype) for a in inputs]
        + [pltpu.SemaphoreType.DMA((8,))],
        compiler_params=pltpu.CompilerParams(vmem_limit_bytes=56 * 1024 * 1024),
    )(*inputs)
    bundle = lax.all_to_all(bundle, "x", 0, 0, tiled=True)

    weight, asked = pl.pallas_call(
        fan_out,
        in_specs=[anywhere],
        out_specs=[whole] * 2,
        out_shape=[
            jax.ShapeDtypeStruct((NY * NZ, 40, 256), bf16),
            jax.ShapeDtypeStruct((NY * NC, 32, HD), bf16),
        ],
        scratch_shapes=[
            pltpu.VMEM((NX, 32, HD), bf16),
            pltpu.SemaphoreType.DMA((1,)),
        ],
        compiler_params=pltpu.CompilerParams(vmem_limit_bytes=8 * 1024 * 1024),
    )(bundle)
    gathered = lax.all_to_all(weight, ("y", "z"), 0, 0, tiled=True)
    left = shift_by(rows, "x", 1)
    right = shift_by(rows, "x", -1)
    far_a = shift_by(left[0:32], "x", 1)
    far_b = shift_by(right[32:64], "x", -1)

    gathered, asked, far_a, far_b = lax.optimization_barrier(
        (gathered.reshape(HALF, 256), asked, far_a, far_b)
    )
    other = shift_by(gathered, "c", 1)
    asked = lax.all_to_all(asked, ("y", "c"), 0, 0, tiled=True)
    rebuilt = pl.pallas_call(
        project,
        in_specs=[anywhere] * 10,
        out_specs=whole,
        out_shape=jax.ShapeDtypeStruct((512, 256), bf16),
        scratch_shapes=[
            pltpu.VMEM((256, 2 * HALF), bf16),
            pltpu.VMEM((NC, HALF, 256), bf16),
            pltpu.VMEM((NX, NY, NC, 80, 256), bf16),
            pltpu.VMEM((64, 2 * HALF), bf16),
            pltpu.VMEM((2, 32, HD), bf16),
            pltpu.VMEM((1, HD), f32),
            pltpu.SemaphoreType.DMA((10,)),
        ],
        compiler_params=pltpu.CompilerParams(vmem_limit_bytes=53 * 1024 * 1024),
        cost_estimate=pl.CostEstimate(
            flops=1400000000, bytes_accessed=8000000, transcendentals=0
        ),
    )(
        rows,
        left,
        far_a,
        far_b,
        right,
        gathered,
        other,
        adapter_down[0].T,
        adapter_up[0],
        key_gain.reshape(1, HD),
    )

    parts = pl.pallas_call(
        attend,
        in_specs=[whole] * 3,
        out_specs=whole,
        out_shape=jax.ShapeDtypeStruct((512, 384), bf16),
        compiler_params=pltpu.CompilerParams(vmem_limit_bytes=16 * 1024 * 1024),
    )(asked, bundle, rebuilt)
    parts = lax.all_to_all(parts.reshape(64, 8, 384), CTX, 0, 0, tiled=True)
    slab, attended = pl.pallas_call(
        merge,
        out_shape=[
            jax.ShapeDtypeStruct((64, 1024), bf16),
            jax.ShapeDtypeStruct((1, 32 * HD), bf16),
        ],
        compiler_params=pltpu.CompilerParams(vmem_limit_bytes=16 * 1024 * 1024),
    )(parts.reshape(512, 384))
    return slab[None], attended[None]


def solution(mesh):
    fine = Mesh(mesh.devices.reshape(NX, NY, NC, NZ), ("x", "y", "c", "z"))
    return jax.shard_map(
        body,
        mesh=fine,
        in_specs=(
            P("z", CTX, None),
            P(CTX + ("z",), None),
            P("z", None, None),
            P("z", None, None, None),
            P(),
            P("z", CTX, None),
            P("z", CTX, None),
            P("z", CTX, None),
            P("z", CTX, None),
            P("z", CTX, None),
            P("z"),
            P("z", CTX),
        ),
        out_specs=(P("z", CTX, None), P("z", CTX, None)),
        check_vma=False,
    )
```
